32 devices in a mesh: dp: 8 (over y, x, core), tensor: 4 (over z).
Axes of the slice: x: 2, y: 2, z: 4, core: 2. Of those that a mesh axis runs over, the one named last changes fastest.
Arguments:
- tokens: bfloat16 [2, 2048, 768], P(None, ('dp', 'tensor')), may hold values from -6 to 6
- encoder: bfloat16 [2, 1024, 768], P(None, ('dp', 'tensor')), may hold values from -6 to 6
- cotangent: bfloat16 [2, 2048, 768], P(None, ('dp', 'tensor')), may hold values from -6 to 6
- dec_segments: int32 [2, 8, 256], P(None, 'dp'), may hold values from 0 to 2, as said below
- enc_segments: int32 [2, 8, 128], P(None, 'dp'), may hold values from 0 to 2, as said below
- buckets: int32 [256], replicated, may hold values from 0 to 31, as said below
- self_query: bfloat16 [768, 768], P('dp', 'tensor'), may hold values from -0.046875 to 0.046875
- self_key: bfloat16 [768, 768], P('dp', 'tensor'), may hold values from -0.21875 to 0.21875
- self_value: bfloat16 [768, 768], P('dp', 'tensor'), may hold values from -0.21875 to 0.21875
- self_output: bfloat16 [768, 768], P('tensor', 'dp'), may hold values from -1.25 to 1.25
- cross_query: bfloat16 [768, 768], P('dp', 'tensor'), may hold values from -0.046875 to 0.046875
- cross_key: bfloat16 [768, 768], P('dp', 'tensor'), may hold values from -0.21875 to 0.21875
- cross_value: bfloat16 [768, 768], P('dp', 'tensor'), may hold values from -0.21875 to 0.21875
- cross_output: bfloat16 [768, 768], P('tensor', 'dp'), may hold values from -1.25 to 1.25
- gate_weight: bfloat16 [768, 2048], P('dp', 'tensor'), may hold values from -0.21875 to 0.21875
- up_weight: bfloat16 [768, 2048], P('dp', 'tensor'), may hold values from -0.21875 to 0.21875
- down_weight: bfloat16 [2048, 768], P('tensor', 'dp'), may hold values from -0.125 to 0.125
- gain_self: bfloat16 [768], P('dp'), may hold values from 0.5 to 1.5
- gain_cross: bfloat16 [768], P('dp'), may hold values from 0.5 to 1.5
- gain_feed: bfloat16 [768], P('dp'), may hold values from 0.5 to 1.5
- bias_table: bfloat16 [32, 12], P(None, 'tensor'), may hold values from -4 to 4
Outputs:
- layer_out: bfloat16 [2, 2048, 768], P(None, ('dp', 'tensor'))
- tokens_grad: float32 [2, 2048, 768], P(None, ('dp', 'tensor'))
- encoder_grad: float32 [2, 1024, 768], P(None, ('dp', 'tensor'))
- self_query_grad: float32 [768, 768], P('dp', 'tensor')
- self_key_grad: float32 [768, 768], P('dp', 'tensor')
- self_value_grad: float32 [768, 768], P('dp', 'tensor')
- self_output_grad: float32 [768, 768], P('tensor', 'dp')
- cross_query_grad: float32 [768, 768], P('dp', 'tensor')
- cross_key_grad: float32 [768, 768], P('dp', 'tensor')
- cross_value_grad: float32 [768, 768], P('dp', 'tensor')
- cross_output_grad: float32 [768, 768], P('tensor', 'dp')
- gate_weight_grad: float32 [768, 2048], P('dp', 'tensor')
- up_weight_grad: float32 [768, 2048], P('dp', 'tensor')
- down_weight_grad: float32 [2048, 768], P('tensor', 'dp')
- gain_self_grad: float32 [768], P(('dp', 'tensor'))
- gain_cross_grad: float32 [768], P(('dp', 'tensor'))
- gain_feed_grad: float32 [768], P(('dp', 'tensor'))
- bias_table_grad: float32 [32, 12], P(None, 'tensor')
The draws below stay inside these ranges and needn't reach their ends.
Inputs may be any that keep to these rules, and one draw needn't show every extreme that they name: `dec_segments`: in each sequence the documents are numbered 0, 1, 2 in order; document 1 begins before position 64 and includes position 192. `enc_segments`: in each encoder row the documents are numbered 0, 1, 2 in order, each with one token or more; document 1 begins before position 64. buckets[d] is the bucket of distance d and never falls as d grows; buckets[d] = d for d < 16, and the last entry is 31.
All inputs are finite; a program needn't handle non-finite values.
Results may differ from the reference program's by a relative error of at most 0.025.
The reference program's roundings to bfloat16 on the way count: a program that leaves them out, or rounds other values in their place, can miss the bound.
Values may be sent and summed in bfloat16 or wider, within the bound.
A program may use at most 128 MiB of HBM per device.

```python
import jax
import jax.numpy as jnp
from jax import lax

D = 768
H = 12
DH = 64
FF = 2048
BUCKETS = 32
SEQ = 256
ENC = 128
MICRO = 2
INNER = 768
SEQS = 8
TOK_MB = 2048
ENC_TOK = 1024


def draw_dec_segments(key, part):
    key = jax.random.fold_in(key, 11)
    first_key, second_key = jax.random.split(key)
    cut_shape = (MICRO, SEQS, 1)
    cut_low = jax.random.randint(first_key, cut_shape, 1, SEQ // 4)
    cut_high = jax.random.randint(second_key, cut_shape, 3 * SEQ // 4 + 1, SEQ)
    position = jnp.arange(SEQ, dtype=jnp.int32)[None, None, :]
    return (position >= cut_low).astype(jnp.int32) + (position >= cut_high).astype(jnp.int32)


def draw_enc_segments(key, part):
    key = jax.random.fold_in(key, 23)
    first_key, second_key = jax.random.split(key)
    cut_shape = (MICRO, SEQS, 1)
    cut_low = jax.random.randint(first_key, cut_shape, 1, ENC // 2)
    cut_high = jax.random.randint(second_key, cut_shape, ENC // 2 + 1, ENC)
    position = jnp.arange(ENC, dtype=jnp.int32)[None, None, :]
    return (position >= cut_low).astype(jnp.int32) + (position >= cut_high).astype(jnp.int32)


def draw_buckets(key, part):
    key = jax.random.fold_in(key, 37)
    position = jnp.arange(SEQ, dtype=jnp.int32)
    stepping = jax.random.randint(key, (SEQ,), 0, 2).astype(jnp.int32)
    stepping = jnp.where(position < BUCKETS // 2, 1, stepping)
    stepping = jnp.where(position == 0, 0, stepping)
    bucket_ids = jnp.minimum(jnp.cumsum(stepping), BUCKETS - 1)
    bucket_ids = jnp.where(position == SEQ - 1, BUCKETS - 1, bucket_ids)
    return bucket_ids.astype(jnp.int32)


def steps_of(stream_key, dims, pieces, least, top_value):
    factor_of, own = 1.0, jax.random.fold_in(stream_key, 6)
    for dim, parts in pieces:
        draws = jnp.exp(jax.random.uniform(jax.random.fold_in(own, dim), (parts,), jnp.float32, least / len(pieces), top_value / len(pieces)))
        factor_of = factor_of * jnp.repeat(draws, dims[dim] // parts).reshape([-1 if axis == dim else 1 for axis in range(len(dims))])
    return factor_of


def bell_draw(stream_key, shape, scale, bound, cuts=(), held_as=jnp.bfloat16):
    factor_of = steps_of(stream_key, shape, cuts, -0.22, 0.18) if cuts else 1.0
    entries = jax.random.normal(stream_key, shape, jnp.float32) * scale * factor_of
    return jnp.minimum(jnp.maximum(entries, -bound), bound).astype(held_as)


def setup_inputs(seed: int = 0) -> dict:
    seeds = jax.random.split(jax.random.key(seed), 22)
    tokens = bell_draw(seeds[0], (MICRO, TOK_MB, D), 1.0, 6.0, ((1, 32),))
    encoder = bell_draw(seeds[1], (MICRO, ENC_TOK, D), 1.0, 6.0, ((1, 32),))
    cotangent = bell_draw(seeds[2], (MICRO, TOK_MB, D), 1.0, 6.0, ((1, 32),))
    dec_segments = draw_dec_segments(jax.random.fold_in(seeds[21], 71), 0)
    enc_segments = draw_enc_segments(jax.random.fold_in(seeds[21], 71), 0)
    buckets = draw_buckets(jax.random.fold_in(seeds[21], 71), 0)
    self_query = bell_draw(seeds[6], (D, INNER), (25 * D) ** -0.5, 0.046875, ((0, 8), (1, 4)))
    self_key = bell_draw(seeds[7], (D, INNER), D ** -0.5, 0.21875, ((0, 8), (1, 4)))
    self_value = bell_draw(seeds[8], (D, INNER), D ** -0.5, 0.21875, ((0, 8), (1, 4)))
    self_output = bell_draw(seeds[9], (INNER, D), (max(INNER // 32, 1)) ** -0.5, 1.25, ((0, 4), (1, 8)))
    cross_query = bell_draw(seeds[10], (D, INNER), (25 * D) ** -0.5, 0.046875, ((0, 8), (1, 4)))
    cross_key = bell_draw(seeds[11], (D, INNER), D ** -0.5, 0.21875, ((0, 8), (1, 4)))
    cross_value = bell_draw(seeds[12], (D, INNER), D ** -0.5, 0.21875, ((0, 8), (1, 4)))
    cross_output = bell_draw(seeds[13], (INNER, D), (max(INNER // 32, 1)) ** -0.5, 1.25, ((0, 4), (1, 8)))
    gate_weight = bell_draw(seeds[14], (D, FF), D ** -0.5, 0.21875, ((0, 8), (1, 4)))
    up_weight = bell_draw(seeds[15], (D, FF), D ** -0.5, 0.21875, ((0, 8), (1, 4)))
    down_weight = bell_draw(seeds[16], (FF, D), FF ** -0.5, 0.125, ((0, 4), (1, 8)))
    gain_self = jnp.clip(1.0 + 0.1 * jax.random.normal(seeds[17], (D,), jnp.float32), 0.5, 1.5).astype(jnp.bfloat16)
    gain_cross = jnp.clip(1.0 + 0.1 * jax.random.normal(seeds[18], (D,), jnp.float32), 0.5, 1.5).astype(jnp.bfloat16)
    gain_feed = jnp.clip(1.0 + 0.1 * jax.random.normal(seeds[19], (D,), jnp.float32), 0.5, 1.5).astype(jnp.bfloat16)
    bias_table = bell_draw(seeds[20], (BUCKETS, H), 1.0, 4.0, ((1, 4),))
    return {"tokens": tokens, "encoder": encoder, "cotangent": cotangent, "dec_segments": dec_segments, "enc_segments": enc_segments, "buckets": buckets, "self_query": self_query, "self_key": self_key, "self_value": self_value, "self_output": self_output, "cross_query": cross_query, "cross_key": cross_key, "cross_value": cross_value, "cross_output": cross_output, "gate_weight": gate_weight, "up_weight": up_weight, "down_weight": down_weight, "gain_self": gain_self, "gain_cross": gain_cross, "gain_feed": gain_feed, "bias_table": bias_table}


@jax.custom_vjp
def reduced_forward(v):
    return lax.optimization_barrier(v.astype(jnp.bfloat16)).astype(jnp.float32)

@jax.custom_vjp
def reduced_backward(v):
    return v

def low_keep(v):
    return (reduced_forward(v), None)

def low_pass(kept, grad):
    return (grad,)

def back_keep(v):
    return (v, None)

def back_low(kept, grad):
    return (reduced_forward(grad),)
reduced_forward.defvjp(low_keep, low_pass)
reduced_backward.defvjp(back_keep, back_low)
EPS = 1e-06
NEG = -1e+30
HIGH = lax.Precision.HIGHEST

def matrix_product(left, right):
    return jnp.dot(left, right, precision=HIGH, preferred_element_type=jnp.float32)

def rms_norm(values, gain_row):
    return values * lax.rsqrt(lax.optimization_barrier(jnp.mean(values * values, axis=-1, keepdims=True)) + EPS) * gain_row

def attention(query_rows, key_rows, value_rows, extra, allowed):
    query_heads = query_rows.reshape(query_rows.shape[0], H, DH)
    key_heads = key_rows.reshape(key_rows.shape[0], H, DH)
    value_heads = value_rows.reshape(value_rows.shape[0], H, DH)
    scores = jnp.einsum('qhd,khd->hqk', query_heads, key_heads, precision=HIGH) + extra
    scores = reduced_backward(scores)
    scores = jnp.where(allowed[None], scores, NEG)
    biggest = lax.optimization_barrier(jnp.max(scores, axis=-1, keepdims=True))
    exponent = jnp.exp(scores - biggest)
    probs = exponent / lax.optimization_barrier(jnp.sum(exponent, axis=-1, keepdims=True))
    mixed = jnp.einsum('hqk,khd->qhd', reduced_forward(probs), value_heads, precision=HIGH)
    return mixed.reshape(query_rows.shape[0], H * DH)

def gelu_tanh(values):
    return jax.nn.gelu(values, approximate=True)

def layer(token_row, encoder_row, parameter_set, dec_seg, enc_seg, bucket_pairs, causal):
    self_query_matrix, self_key_matrix, self_value_matrix, self_output_matrix, cross_query_matrix, cross_key_matrix, cross_value_matrix, cross_output_matrix, gate_projection_weight, up_projection_weight, down_projection_weight, self_norm_gain, cross_norm_gain, feed_norm_gain, bias_table_whole = parameter_set
    self_normed_rows = reduced_forward(rms_norm(token_row, self_norm_gain))
    query1 = reduced_backward(reduced_forward(matrix_product(self_normed_rows, self_query_matrix)))
    self_key_heads = reduced_backward(reduced_forward(matrix_product(self_normed_rows, self_key_matrix)))
    value1 = reduced_backward(reduced_forward(matrix_product(self_normed_rows, self_value_matrix)))
    bias_full = jnp.transpose(bias_table_whole[bucket_pairs], (2, 0, 1))
    allowed1 = causal & (dec_seg[:, None] == dec_seg[None, :])
    mixed1 = reduced_backward(reduced_forward(attention(query1, self_key_heads, value1, bias_full, allowed1)))
    first = token_row + reduced_backward(matrix_product(mixed1, self_output_matrix))
    normed2 = reduced_forward(rms_norm(first, cross_norm_gain))
    query2 = reduced_backward(reduced_forward(matrix_product(normed2, cross_query_matrix)))
    key2 = reduced_backward(reduced_forward(matrix_product(encoder_row, cross_key_matrix)))
    value2 = reduced_backward(reduced_forward(matrix_product(encoder_row, cross_value_matrix)))
    allowed2 = dec_seg[:, None] == enc_seg[None, :]
    mixed2 = reduced_backward(reduced_forward(attention(query2, key2, value2, 0.0, allowed2)))
    second = first + reduced_backward(matrix_product(mixed2, cross_output_matrix))
    normed3 = reduced_forward(rms_norm(second, feed_norm_gain))
    gate_pre = reduced_backward(matrix_product(normed3, gate_projection_weight))
    up_pre = reduced_backward(matrix_product(normed3, up_projection_weight))
    hidden = reduced_forward(gelu_tanh(gate_pre) * up_pre)
    return second + reduced_backward(matrix_product(hidden, down_projection_weight))

def reference(tokens, encoder, cotangent, dec_segments, enc_segments, buckets, self_query, self_key, self_value, self_output, cross_query, cross_key, cross_value, cross_output, gate_weight, up_weight, down_weight, gain_self, gain_cross, gain_feed, bias_table):
    parameter_set = tuple((w.astype(jnp.float32) for w in (self_query, self_key, self_value, self_output, cross_query, cross_key, cross_value, cross_output, gate_weight, up_weight, down_weight, gain_self, gain_cross, gain_feed, bias_table)))
    seq_count = MICRO * SEQS
    token_rows = tokens.astype(jnp.float32).reshape(seq_count, SEQ, D)
    encoder_rows = encoder.astype(jnp.float32).reshape(seq_count, ENC, D)
    cot_rows = cotangent.astype(jnp.float32).reshape(seq_count, SEQ, D)
    dec_rows = dec_segments.reshape(seq_count, SEQ).astype(jnp.int32)
    enc_rows = enc_segments.reshape(seq_count, ENC).astype(jnp.int32)
    position = jnp.arange(SEQ, dtype=jnp.int32)
    distance = jnp.clip(position[:, None] - position[None, :], 0, SEQ - 1).astype(jnp.int32)
    bucket_pairs = buckets.astype(jnp.int32)[distance]
    causal = position[:, None] >= position[None, :]
    zero_grads = tuple((jnp.zeros_like(p) for p in parameter_set))

    def visit(totals, record):
        token_row, encoder_row, cot_row, dec_seg, enc_seg = record

        def run_layer(tok_in, enc_in, par_in):
            return layer(tok_in, enc_in, par_in, dec_seg, enc_seg, bucket_pairs, causal)
        result, pullback = jax.vjp(run_layer, token_row, encoder_row, parameter_set)
        tok_grad, enc_grad, par_grad = pullback(cot_row)
        totals = tuple((a + b for a, b in zip(totals, par_grad)))
        return (totals, (result.astype(jnp.bfloat16), tok_grad, enc_grad))
    totals, (results, tok_grads, enc_grads) = lax.scan(visit, zero_grads, (token_rows, encoder_rows, cot_rows, dec_rows, enc_rows))
    return (results.reshape(MICRO, SEQS * SEQ, D), tok_grads.reshape(MICRO, SEQS * SEQ, D), enc_grads.reshape(MICRO, SEQS * ENC, D), totals[0], totals[1], totals[2], totals[3], totals[4], totals[5], totals[6], totals[7], totals[8], totals[9], totals[10], totals[11], totals[12], totals[13], totals[14])
```

```python
import functools

import jax
import jax.numpy as jnp
from jax import lax
from jax.experimental import pallas as pl
from jax.experimental.pallas import tpu as pltpu
from jax.sharding import PartitionSpec as P

BUCKETS = 32
EPS = 1e-06
NEG = -1e30
MESH = pl.DeviceIdType.MESH
CUBE = 8
VMEM_LIMIT = 56 * 1024 * 1024


def run_together(*streams):
    streams = list(streams)
    while streams:
        for stream in list(streams):
            try:
                next(stream)
            except StopIteration:
                streams.remove(stream)


def greet(pos, count, cube_me):
    barrier = pltpu.get_barrier_semaphore()

    @pl.when(pos > 0)
    def _():
        pl.semaphore_signal(barrier, inc=1, device_id={"tensor": pos - 1}, device_id_type=MESH)

    @pl.when(pos < count - 1)
    def _():
        pl.semaphore_signal(barrier, inc=1, device_id={"tensor": pos + 1}, device_id_type=MESH)

    waits = 2 - jnp.where(pos == 0, 1, 0) - jnp.where(pos == count - 1, 1, 0)
    if cube_me is not None:
        for flip in (1, 2, 4):
            pl.semaphore_signal(
                barrier, inc=1, device_id={"dp": cube_me ^ flip}, device_id_type=MESH
            )
        waits = waits + 3
    pl.semaphore_wait(barrier, waits)


def line_gather(pos, count, buf, send, recv):
    micro = buf.shape[0]
    rows = buf.shape[1] // count

    def piece(block, step):
        return buf.at[step, pl.ds(pl.multiple_of(block * rows, rows), rows)]

    def copy(block, step, target, way):
        return pltpu.make_async_remote_copy(
            src_ref=piece(block, step),
            dst_ref=piece(block, step),
            send_sem=send.at[way, block, step],
            recv_sem=recv.at[block, step],
            device_id={"tensor": target},
            device_id_type=MESH,
        )

    for hop in range(count):
        for step in range(micro):
            for way, target, block, can_send in (
                (0, pos + 1, pos - hop, pos < count - 1),
                (1, pos - 1, pos + hop, pos > 0),
            ):
                there = (block >= 0) & (block < count)

                if hop > 0:

                    @pl.when(there)
                    def _(block=block, step=step, way=way, target=target):
                        copy(block, step, target, way).wait_recv()

                if hop < count - 1:

                    @pl.when(there & can_send)
                    def _(block=block, step=step, way=way, target=target):
                        copy(block, step, target, way).start()

        yield
    for hop in range(count - 1):
        for step in range(micro):
            for way, target, block, can_send in (
                (0, pos + 1, pos - hop, pos < count - 1),
                (1, pos - 1, pos + hop, pos > 0),
            ):

                @pl.when((block >= 0) & (block < count) & can_send)
                def _(block=block, step=step, way=way, target=target):
                    copy(block, step, target, way).wait_send()


def line_scatter(pos, count, parts, got, staged, total, send, recv):
    micro = parts.shape[0]
    rows = parts.shape[1] // count

    def at(block):
        return pl.ds(pl.multiple_of(block * rows, rows), rows)

    def copy(block, step, target, way):
        return pltpu.make_async_remote_copy(
            src_ref=staged.at[way, step, at(block)],
            dst_ref=got.at[way, step, at(block)],
            send_sem=send.at[way, block, step],
            recv_sem=recv.at[way, block, step],
            device_id={"tensor": target},
            device_id_type=MESH,
        )

    def ways(hop):
        return (
            (0, pos + 1, pos + hop, pos + hop < count, pos > 0),
            (1, pos - 1, pos - hop, pos - hop >= 0, pos < count - 1),
        )

    for hop in range(count - 1, 0, -1):
        for step in range(micro):
            for way, target, block, there, has_input in ways(hop):

                @pl.when(there & has_input)
                def _(way=way, target=target, block=block, step=step):
                    copy(block, step, target, way).wait_recv()
                    staged[way, step, at(block)] = (
                        parts[step, at(block)].astype(jnp.float32)
                        + got[way, step, at(block)].astype(jnp.float32)
                    ).astype(staged.dtype)
                    copy(block, step, target, way).start()

                @pl.when(there & jnp.logical_not(has_input))
                def _(way=way, target=target, block=block, step=step):
                    staged[way, step, at(block)] = parts[step, at(block)]
                    copy(block, step, target, way).start()

        yield
    for step in range(micro):
        total[step] = parts[step, at(pos)].astype(jnp.float32)
        for way, target, block, there, has_input in ways(0):

            @pl.when(has_input)
            def _(way=way, target=target, step=step):
                copy(pos, step, target, way).wait_recv()
                total[step] = total[step] + got[way, step, at(pos)].astype(jnp.float32)

    for hop in range(count - 1, 0, -1):
        for step in range(micro):
            for way, target, block, there, has_input in ways(hop):

                @pl.when(there)
                def _(way=way, target=target, block=block, step=step):
                    copy(block, step, target, way).wait_send()


def cube_gather(me, buf, send, recv):
    half_rows = buf.shape[1] // 2

    def copy(block, half, flip, slot):
        piece = buf.at[block, pl.ds(half * half_rows, half_rows)]
        return pltpu.make_async_remote_copy(
            src_ref=piece,
            dst_ref=piece,
            send_sem=send.at[slot, half],
            recv_sem=recv.at[block, half],
            device_id={"dp": me ^ flip},
            device_id_type=MESH,
        )

    started = []

    def begin(block, half, flip):
        one = copy(block, half, flip, len(started) // 2 if half == 0 else len(started) // 2)
        one.start()
        started.append(one)

    firsts = ((2, 4), (4, 2))
    for half in range(2):
        begin(me, half, firsts[half][0])
    for half in range(2):
        begin(me, half, firsts[half][1])
    for half in range(2):
        begin(me, half, 1)
    yield
    for half in range(2):
        first, second = firsts[half]
        copy(me ^ first, half, first, 0).wait_recv()
        begin(me ^ first, half, second)
    for half in range(2):
        begin(me ^ firsts[half][0], half, 1)
    yield
    for half in range(2):
        copy(me ^ firsts[half][1], half, firsts[half][1], 0).wait_recv()
        begin(me ^ firsts[half][1], half, 1)
    yield
    for half in range(2):
        copy(me ^ 6, half, firsts[half][1], 0).wait_recv()
        begin(me ^ 6, half, 1)
    yield
    for other in (0, 2, 4, 6):
        for half in range(2):
            copy(me ^ 1 ^ other, half, 1, 0).wait_recv()
    for one in started:
        one.wait_send()


def cube_scatter(me, parts, got1, sums, got2, got3, total, send1, recv1, send2, recv2, send3, recv3):
    half_rows = parts.shape[1] // 2
    firsts = ((2, 4), (4, 2))

    def rows_of(half):
        return pl.ds(half * half_rows, half_rows)

    def one_copy(src, dst, send, recv, flip):
        return pltpu.make_async_remote_copy(
            src_ref=src,
            dst_ref=dst,
            send_sem=send,
            recv_sem=recv,
            device_id={"dp": me ^ flip},
            device_id_type=MESH,
        )

    first_copies = {}
    for slot in (3, 1, 2, 0):
        first_copies[slot] = one_copy(
            parts.at[me ^ 1 ^ (2 * slot)], got1.at[slot], send1.at[slot], recv1.at[slot], 1
        )
        first_copies[slot].start()
    yield
    second_copies = {}
    for slot in (3, 1, 2, 0):
        first_copies[slot].wait_recv()
        sums[slot] = (
            parts[me ^ (2 * slot)].astype(jnp.float32) + got1[slot].astype(jnp.float32)
        ).astype(sums.dtype)
        for half in range(2):
            first, second = firsts[half]
            if slot == 3 or slot == first // 2:
                goes = 1 if slot == 3 else 0
                second_copies[half, goes] = one_copy(
                    sums.at[slot, rows_of(half)],
                    got2.at[half, goes],
                    send2.at[half, goes],
                    recv2.at[half, goes],
                    first,
                )
                second_copies[half, goes].start()
    yield
    third_copies = {}
    for half in range(2):
        first, second = firsts[half]
        second_copies[half, 1].wait_recv()
        slot = second // 2
        sums[slot, rows_of(half)] = (
            sums[slot, rows_of(half)].astype(jnp.float32) + got2[half, 1].astype(jnp.float32)
        ).astype(sums.dtype)
        third_copies[half] = one_copy(
            sums.at[slot, rows_of(half)], got3.at[half], send3.at[half], recv3.at[half], second
        )
        third_copies[half].start()
    yield
    for half in range(2):
        second_copies[half, 0].wait_recv()
        total[rows_of(half)] = sums[0, rows_of(half)].astype(jnp.float32) + got2[half, 0].astype(
            jnp.float32
        )
    yield
    for half in range(2):
        third_copies[half].wait_recv()
        total[rows_of(half)] = total[rows_of(half)] + got3[half].astype(jnp.float32)
    for group in (first_copies, second_copies, third_copies):
        for one in group.values():
            one.wait_send()


def norm_forward(values, gain_row):
    inv_root = lax.rsqrt(jnp.mean(values * values, axis=-1, keepdims=True) + EPS)
    return values * inv_root * gain_row


def norm_backward(grad_out, values, gain_row):
    inv_root = lax.rsqrt(jnp.mean(values * values, axis=-1, keepdims=True) + EPS)
    normal = values * inv_root
    scaled = grad_out * gain_row
    values_grad = inv_root * (scaled - normal * jnp.mean(scaled * normal, axis=-1, keepdims=True))
    return (values_grad, jnp.sum(grad_out * normal, axis=0, keepdims=True))


def own_rows(pos, buf, count):
    rows = buf.shape[1] // count
    return pl.ds(pl.multiple_of(pos * rows, rows), rows)


def scatter_scratch(shape):
    return [
        pltpu.VMEM((2,) + shape, jnp.bfloat16),
        pltpu.VMEM((2,) + shape, jnp.bfloat16),
    ]


def scatter_sems(count, micro):
    return [
        pltpu.SemaphoreType.DMA((2, count, micro)),
        pltpu.SemaphoreType.DMA((2, count, micro)),
    ]


def gather_sems(count, micro):
    return [
        pltpu.SemaphoreType.DMA((2, count, micro)),
        pltpu.SemaphoreType.DMA((count, micro)),
    ]


def call(kernel, outs, scratch, ident, name, *args):
    return pl.pallas_call(
        kernel,
        out_shape=[jax.ShapeDtypeStruct(shape, kind) for shape, kind in outs],
        in_specs=[pl.BlockSpec(memory_space=pltpu.VMEM)] * len(args),
        out_specs=[pl.BlockSpec(memory_space=pltpu.VMEM)] * len(outs),
        scratch_shapes=scratch,
        compiler_params=pltpu.CompilerParams(
            collective_id=ident, has_side_effects=True, vmem_limit_bytes=VMEM_LIMIT
        ),
        name=name,
    )(*args)


def entry_kernel(count, with_cube, *refs):
    if with_cube:
        weights, refs = refs[0], refs[1:]
    rows_in, refs = refs[:3], refs[3:]
    if with_cube:
        weights_all, refs = refs[0], refs[1:]
    rows_out, refs = refs[:3], refs[3:]
    pos = lax.axis_index("tensor")
    me = lax.axis_index("dp") if with_cube else None
    for source, target in zip(rows_in, rows_out):
        for step in range(source.shape[0]):
            target[step, own_rows(pos, target, count)] = source[step]
    if with_cube:
        weights_all[me] = weights[...]
    greet(pos, count, me)
    streams = []
    if with_cube:
        streams.append(cube_gather(me, weights_all, refs[6], refs[7]))

    def lines():
        for which in range(3):
            yield from line_gather(
                pos, count, rows_out[which], refs[2 * which], refs[2 * which + 1]
            )

    run_together(*streams, lines())


def forward_kernel(
    count, parts, resid, gain, total_out, normed_all, got, staged, s_send, s_recv, g_send, g_recv
):
    pos = lax.axis_index("tensor")
    greet(pos, count, None)
    run_together(line_scatter(pos, count, parts, got, staged, total_out, s_send, s_recv))
    for step in range(parts.shape[0]):
        total = total_out[step] + resid[step].astype(jnp.float32)
        total_out[step] = total
        normed_all[step, own_rows(pos, normed_all, count)] = norm_forward(total, gain[...]).astype(
            jnp.bfloat16
        )
    run_together(line_gather(pos, count, normed_all, g_send, g_recv))


def back_kernel(
    count,
    side_kind,
    parts,
    side_parts,
    values,
    gain,
    grad_in,
    side_resid,
    grad_out,
    gathered,
    side_out,
    gain_out,
    got,
    staged,
    side_got,
    side_staged,
    side_total,
    s_send,
    s_recv,
    t_send,
    t_recv,
    g_send,
    g_recv,
):
    pos = lax.axis_index("tensor")
    greet(pos, count, None)

    def main():
        yield from line_scatter(pos, count, parts, got, staged, grad_out, s_send, s_recv)
        gain_out[...] = jnp.zeros_like(gain_out)
        for step in range(parts.shape[0]):
            moved, gain_part = norm_backward(grad_out[step], values[step], gain[...])
            total = grad_in[step].astype(jnp.float32) + moved
            grad_out[step] = total
            gain_out[...] = gain_out[...] + gain_part
            gathered[step, own_rows(pos, gathered, count)] = total.astype(jnp.bfloat16)
        yield from line_gather(pos, count, gathered, g_send, g_recv)

    def side():
        yield from line_scatter(
            pos, count, side_parts, side_got, side_staged, side_total, t_send, t_recv
        )
        for step in range(parts.shape[0]):
            if side_kind == "out":
                side_out[step] = (side_total[step] + side_resid[step]).astype(jnp.bfloat16)
            else:
                side_out[step] = side_total[step]

    run_together(main(), side())


def exit_kernel(count, with_cube, *refs):
    parts, values, gain, grad_in = refs[:4]
    refs = refs[4:]
    if with_cube:
        weight_parts, refs = refs[0], refs[1:]
    grad_out, gain_out = refs[:2]
    refs = refs[2:]
    if with_cube:
        weight_out, refs = refs[0], refs[1:]
    got, staged, s_send, s_recv = refs[:4]
    refs = refs[4:]
    pos = lax.axis_index("tensor")
    me = lax.axis_index("dp") if with_cube else None
    greet(pos, count, me)

    def main():
        yield from line_scatter(pos, count, parts, got, staged, grad_out, s_send, s_recv)
        gain_out[...] = jnp.zeros_like(gain_out)
        for step in range(parts.shape[0]):
            moved, gain_part = norm_backward(
                grad_out[step], values[step].astype(jnp.float32), gain[...]
            )
            grad_out[step] = grad_in[step] + moved
            gain_out[...] = gain_out[...] + gain_part

    streams = [main()]
    if with_cube:
        got1, sums, got2, got3 = refs[:4]
        streams.insert(
            0, cube_scatter(me, weight_parts, got1, sums, got2, got3, weight_out, *refs[4:])
        )
    run_together(*streams)


def dot_plain(left, right):
    return jnp.dot(left, right, preferred_element_type=jnp.float32)


def dot_left_t(left, right):
    return lax.dot_general(
        left, right, (((0,), (0,)), ((), ())), preferred_element_type=jnp.float32
    )


def dot_right_t(left, right):
    return lax.dot_general(
        left, right, (((1,), (1,)), ((), ())), preferred_element_type=jnp.float32
    )


def gelu_tanh(values):
    return jax.nn.gelu(values, approximate=True)


def head_split(values, heads_local):
    return values.reshape(values.shape[:2] + (heads_local, values.shape[2] // heads_local))


def attend_forward(query_rows, key_rows, value_rows, heads_local, extra, allowed):
    scores = (
        jnp.einsum(
            "bqhd,bkhd->bhqk",
            head_split(query_rows, heads_local),
            head_split(key_rows, heads_local),
            preferred_element_type=jnp.float32,
        )
        + extra
    )
    scores = jnp.where(allowed[:, None], scores, NEG)
    biggest = jnp.max(scores, axis=-1, keepdims=True)
    exponent = jnp.exp(scores - biggest)
    probs = exponent / jnp.sum(exponent, axis=-1, keepdims=True)
    mixed = jnp.einsum(
        "bhqk,bkhd->bqhd",
        probs.astype(jnp.bfloat16),
        head_split(value_rows, heads_local),
        preferred_element_type=jnp.float32,
    )
    return (mixed.reshape(query_rows.shape).astype(jnp.bfloat16), probs)


def attend_backward(query_rows, key_rows, value_rows, heads_local, probs, mixed_grad):
    grad_heads = head_split(mixed_grad, heads_local)
    query_heads = head_split(query_rows, heads_local)
    key_heads = head_split(key_rows, heads_local)
    prob_grad = jnp.einsum(
        "bqhd,bkhd->bhqk",
        grad_heads,
        head_split(value_rows, heads_local),
        preferred_element_type=jnp.float32,
    )
    score_low = (probs * (prob_grad - jnp.sum(probs * prob_grad, axis=-1, keepdims=True))).astype(
        jnp.bfloat16
    )
    query_grad = jnp.einsum(
        "bhqk,bkhd->bqhd", score_low, key_heads, preferred_element_type=jnp.float32
    )
    key_grad = jnp.einsum(
        "bhqk,bqhd->bkhd", score_low, query_heads, preferred_element_type=jnp.float32
    )
    value_grad = jnp.einsum(
        "bhqk,bqhd->bkhd", probs.astype(jnp.bfloat16), grad_heads, preferred_element_type=jnp.float32
    )
    return (
        query_grad.reshape(query_rows.shape).astype(jnp.bfloat16),
        key_grad.reshape(key_rows.shape).astype(jnp.bfloat16),
        value_grad.reshape(key_rows.shape).astype(jnp.bfloat16),
        score_low,
    )


def rows_dot(rows, matrix):
    return lax.dot_general(
        rows, matrix, (((2,), (0,)), ((), ())), preferred_element_type=jnp.float32
    )


def rows_dot_t(rows, matrix):
    return lax.dot_general(
        rows, matrix, (((2,), (1,)), ((), ())), preferred_element_type=jnp.float32
    )


def weight_dot(left, right):
    return dot_left_t(
        left.reshape(-1, left.shape[-1]), right.reshape(-1, right.shape[-1])
    ).astype(jnp.bfloat16)

def toeplitz_bias(bucket_low, table_local):
    per_distance = jnp.dot(bucket_low, table_local, preferred_element_type=jnp.float32)
    length = per_distance.shape[0]
    reversed_rows = jnp.concatenate(
        [per_distance[::-1].T, jnp.zeros((per_distance.shape[1], length), jnp.float32)], axis=1
    )
    tiled_rows = jnp.tile(reversed_rows, (1, length))
    skewed = tiled_rows[:, : length * (2 * length - 1)].reshape(-1, length, 2 * length - 1)
    return skewed[:, :, length - 1 :]


def table_back(score_low, bucket_float):
    heads_local = score_low.shape[0]
    length = score_low.shape[1]
    padded = jnp.concatenate(
        [jnp.zeros((heads_local, length, length - 1), jnp.float32), score_low.astype(jnp.float32)],
        axis=2,
    )
    flat_rows = jnp.concatenate(
        [padded.reshape(heads_local, -1), jnp.zeros((heads_local, length), jnp.float32)], axis=1
    )
    folded = jnp.sum(flat_rows.reshape(heads_local, length, 2 * length), axis=1)
    per_distance = folded[:, :length][:, ::-1].T
    return dot_left_t(bucket_float, per_distance)


def body(
    tokens,
    encoder,
    cotangent,
    dec_segments,
    enc_segments,
    buckets,
    self_query,
    self_key,
    self_value,
    self_output,
    cross_query,
    cross_key,
    cross_value,
    cross_output,
    gate_weight,
    up_weight,
    down_weight,
    gain_self,
    gain_cross,
    gain_feed,
    bias_table,
):
    low = jnp.bfloat16
    dp_count = lax.axis_size("dp")
    count = lax.axis_size("tensor")
    heads_local = bias_table.shape[1]
    inner = self_query.shape[1]
    hidden_local = gate_weight.shape[1]
    shard_rows = self_query.shape[0]
    width = shard_rows * dp_count
    micro, row_count = tokens.shape[:2]
    seq_len = row_count * count
    enc_len = encoder.shape[1] * count
    with_cube = dp_count == CUBE and shard_rows % 32 == 0

    gain_columns = jnp.pad(
        jnp.stack([gain_self, gain_cross, gain_feed], axis=1), ((0, 0), (0, 125))
    )
    packed = jnp.concatenate(
        [
            gate_weight,
            up_weight,
            down_weight.T,
            self_query,
            self_key,
            self_value,
            cross_query,
            cross_key,
            cross_value,
            self_output.T,
            cross_output.T,
            gain_columns,
        ],
        axis=1,
    )
    rows_shape = (micro, seq_len, width)
    enc_shape = (micro, enc_len, width)
    own_shape = (micro, row_count, width)
    line_sems = gather_sems(count, micro)
    entry_args = [tokens, cotangent, encoder]
    entry_outs = [(rows_shape, low), (rows_shape, low), (enc_shape, low)]
    entry_scratch = line_sems * 3
    if with_cube:
        entry_args.insert(0, packed)
        entry_outs.insert(0, ((CUBE,) + packed.shape, low))
        entry_scratch = entry_scratch + [
            pltpu.SemaphoreType.DMA((8, 2)),
            pltpu.SemaphoreType.DMA((CUBE, 2)),
        ]
    entry = call(
        functools.partial(entry_kernel, count, with_cube),
        entry_outs,
        entry_scratch,
        0,
        "entry_gather",
        *entry_args,
    )
    if with_cube:
        whole, tokens_all, cot_all, encoder_all = entry
        whole = whole.reshape(width, packed.shape[1])
    else:
        tokens_all, cot_all, encoder_all = entry
        whole = lax.all_gather(packed, "dp", axis=0, tiled=True)
    w_gate_up = whole[:, : 2 * hidden_local]
    w_down_t = whole[:, 2 * hidden_local : 3 * hidden_local]
    base = 3 * hidden_local
    w_qkv = whole[:, base : base + 3 * inner]
    w_cq = whole[:, base + 3 * inner : base + 4 * inner]
    w_ckv = whole[:, base + 4 * inner : base + 6 * inner]
    w_so_t = whole[:, base + 6 * inner : base + 7 * inner]
    w_co_t = whole[:, base + 7 * inner : base + 8 * inner]
    gains = whole[:, base + 8 * inner : base + 8 * inner + 3].T.astype(jnp.float32)
    gain1, gain2, gain3 = gains[0:1], gains[1:2], gains[2:3]

    position = jnp.arange(seq_len, dtype=jnp.int32)
    causal = position[:, None] >= position[None, :]
    bucket_hits = buckets[:, None] == jnp.arange(BUCKETS, dtype=jnp.int32)[None, :]
    bias_full = toeplitz_bias(bucket_hits.astype(low), bias_table)
    dec_seg = dec_segments[:, 0]
    enc_seg = enc_segments[:, 0]
    self_allowed = causal[None] & (dec_seg[:, :, None] == dec_seg[:, None, :])
    cross_allowed = dec_seg[:, :, None] == enc_seg[:, None, :]

    forward_scratch = (
        scatter_scratch(rows_shape) + scatter_sems(count, micro) + gather_sems(count, micro)
    )
    normed1_all = norm_forward(tokens_all.astype(jnp.float32), gain1).astype(low)
    qkv = rows_dot(normed1_all, w_qkv).astype(low)
    query1, key1, value1 = (
        qkv[..., :inner],
        qkv[..., inner : 2 * inner],
        qkv[..., 2 * inner :],
    )
    mixed1, probs1 = attend_forward(query1, key1, value1, heads_local, bias_full, self_allowed)
    first, normed2_all = call(
        functools.partial(forward_kernel, count),
        [(own_shape, jnp.float32), (rows_shape, low)],
        forward_scratch,
        1,
        "self_sum_norm",
        rows_dot_t(mixed1, w_so_t).astype(low),
        tokens,
        gain2,
    )
    key_value2 = rows_dot(encoder_all, w_ckv).astype(low)
    key2, value2 = key_value2[..., :inner], key_value2[..., inner:]
    query2 = rows_dot(normed2_all, w_cq).astype(low)
    mixed2, probs2 = attend_forward(query2, key2, value2, heads_local, 0.0, cross_allowed)
    second, normed3_all = call(
        functools.partial(forward_kernel, count),
        [(own_shape, jnp.float32), (rows_shape, low)],
        forward_scratch,
        2,
        "cross_sum_norm",
        rows_dot_t(mixed2, w_co_t).astype(low),
        first,
        gain3,
    )
    gate_up = rows_dot(normed3_all, w_gate_up)
    gate_pre, up_pre = gate_up[..., :hidden_local], gate_up[..., hidden_local:]
    gate_act, gate_pull = jax.vjp(gelu_tanh, gate_pre)
    hidden = (gate_act * up_pre).astype(low)
    hidden_grad = rows_dot(cot_all, w_down_t)
    gate_grad = gate_pull(hidden_grad * up_pre)[0].astype(low)
    up_grad = (hidden_grad * gate_act).astype(low)
    gate_up_grad = jnp.concatenate([gate_grad, up_grad], axis=-1)

    def back_scratch(side_shape, side_own):
        return (
            scatter_scratch(rows_shape)
            + scatter_scratch(side_shape)
            + [pltpu.VMEM(side_own, jnp.float32)]
            + scatter_sems(count, micro) * 2
            + gather_sems(count, micro)
        )

    second_grad, cross_out_all, layer_out, gain3_part = call(
        functools.partial(back_kernel, count, "out"),
        [
            (own_shape, jnp.float32),
            (rows_shape, low),
            (own_shape, low),
            ((1, width), jnp.float32),
        ],
        back_scratch(rows_shape, own_shape),
        3,
        "feed_back",
        rows_dot_t(gate_up_grad, w_gate_up).astype(low),
        rows_dot_t(hidden, w_down_t).astype(low),
        second,
        gain3,
        cotangent,
        second,
    )
    mixed2_grad = rows_dot(cross_out_all, w_co_t).astype(low)
    query2_grad, key2_grad, value2_grad, score2_low = attend_backward(
        query2, key2, value2, heads_local, probs2, mixed2_grad
    )
    key_value2_grad = jnp.concatenate([key2_grad, value2_grad], axis=-1)
    enc_own = (micro, encoder.shape[1], width)
    first_grad, self_out_all, encoder_grad, gain2_part = call(
        functools.partial(back_kernel, count, "plain"),
        [
            (own_shape, jnp.float32),
            (rows_shape, low),
            (enc_own, jnp.float32),
            ((1, width), jnp.float32),
        ],
        back_scratch(enc_shape, enc_own),
        4,
        "cross_back",
        rows_dot_t(query2_grad, w_cq).astype(low),
        rows_dot_t(key_value2_grad, w_ckv).astype(low),
        first,
        gain2,
        second_grad,
        second,
    )
    mixed1_grad = rows_dot(self_out_all, w_so_t).astype(low)
    query1_grad, key1_grad, value1_grad, score1_low = attend_backward(
        query1, key1, value1, heads_local, probs1, mixed1_grad
    )
    qkv_grad = jnp.concatenate([query1_grad, key1_grad, value1_grad], axis=-1)
    weight_parts = jnp.concatenate(
        [
            weight_dot(normed3_all, gate_up_grad),
            weight_dot(cot_all, hidden),
            weight_dot(normed1_all, qkv_grad),
            weight_dot(normed2_all, query2_grad),
            weight_dot(encoder_all, key_value2_grad),
            weight_dot(self_out_all, mixed1),
            weight_dot(cross_out_all, mixed2),
        ],
        axis=1,
    )
    columns = weight_parts.shape[1]
    exit_args = [rows_dot_t(qkv_grad, w_qkv).astype(low), tokens, gain1, first_grad]
    exit_outs = [(own_shape, jnp.float32), ((1, width), jnp.float32)]
    exit_scratch = scatter_scratch(rows_shape) + scatter_sems(count, micro)
    if with_cube:
        exit_args.append(weight_parts.reshape(CUBE, shard_rows, columns))
        exit_outs.append(((shard_rows, columns), jnp.float32))
        exit_scratch = exit_scratch + [
            pltpu.VMEM((4, shard_rows, columns), low),
            pltpu.VMEM((4, shard_rows, columns), low),
            pltpu.VMEM((2, 2, shard_rows // 2, columns), low),
            pltpu.VMEM((2, shard_rows // 2, columns), low),
            pltpu.SemaphoreType.DMA((4,)),
            pltpu.SemaphoreType.DMA((4,)),
            pltpu.SemaphoreType.DMA((2, 2)),
            pltpu.SemaphoreType.DMA((2, 2)),
            pltpu.SemaphoreType.DMA((2,)),
            pltpu.SemaphoreType.DMA((2,)),
        ]
    ended = call(
        functools.partial(exit_kernel, count, with_cube),
        exit_outs,
        exit_scratch,
        5,
        "exit_sums",
        *exit_args,
    )
    if with_cube:
        token_grad, gain1_part, owned = ended
    else:
        token_grad, gain1_part = ended
        owned = lax.psum_scatter(
            weight_parts.astype(jnp.float32), "dp", scatter_dimension=0, tiled=True
        )
    tables = table_back(jnp.sum(score1_low.astype(jnp.float32), axis=0), bucket_hits.astype(jnp.float32))
    pos = lax.axis_index("tensor")
    placed_table = jnp.where(
        (jnp.arange(count, dtype=jnp.int32) == pos)[:, None, None], tables[None], 0.0
    )
    small = jnp.concatenate(
        [
            gain1_part.reshape(-1),
            gain2_part.reshape(-1),
            gain3_part.reshape(-1),
            placed_table.reshape(-1),
        ]
    )
    small = lax.psum(small, ("dp", "tensor"))
    index = lax.axis_index("dp") * count + pos
    piece = width // (dp_count * count)
    gain_grads = tuple(
        lax.dynamic_slice(small, (which * width + index * piece,), (piece,)) for which in range(3)
    )
    table_size = tables.shape[0] * tables.shape[1]
    table_grad = lax.dynamic_slice(small, (3 * width + pos * table_size,), (table_size,)).reshape(
        tables.shape
    )

    def wide(start, size):
        return owned[:, start : start + size]

    return (
        layer_out,
        token_grad,
        encoder_grad,
        wide(base, inner),
        wide(base + inner, inner),
        wide(base + 2 * inner, inner),
        wide(base + 6 * inner, inner).T,
        wide(base + 3 * inner, inner),
        wide(base + 4 * inner, inner),
        wide(base + 5 * inner, inner),
        wide(base + 7 * inner, inner).T,
        wide(0, hidden_local),
        wide(hidden_local, hidden_local),
        wide(2 * hidden_local, hidden_local).T,
    ) + gain_grads + (table_grad,)


def solution(mesh):
    placed = (
        P(None, ("dp", "tensor"), None),
        P(None, ("dp", "tensor"), None),
        P(None, ("dp", "tensor"), None),
        P(None, "dp", None),
        P(None, "dp", None),
        P(),
        P("dp", "tensor"),
        P("dp", "tensor"),
        P("dp", "tensor"),
        P("tensor", "dp"),
        P("dp", "tensor"),
        P("dp", "tensor"),
        P("dp", "tensor"),
        P("tensor", "dp"),
        P("dp", "tensor"),
        P("dp", "tensor"),
        P("tensor", "dp"),
        P("dp"),
        P("dp"),
        P("dp"),
        P(None, "tensor"),
    )
    return jax.shard_map(
        body,
        mesh=mesh,
        in_specs=placed,
        out_specs=(
            P(None, ("dp", "tensor"), None),
            P(None, ("dp", "tensor"), None),
            P(None, ("dp", "tensor"), None),
            P("dp", "tensor"),
            P("dp", "tensor"),
            P("dp", "tensor"),
            P("tensor", "dp"),
            P("dp", "tensor"),
            P("dp", "tensor"),
            P("dp", "tensor"),
            P("tensor", "dp"),
            P("dp", "tensor"),
            P("dp", "tensor"),
            P("tensor", "dp"),
            P(("dp", "tensor")),
            P(("dp", "tensor")),
            P(("dp", "tensor")),
            P(None, "tensor"),
        ),
        check_vma=False,
    )
```

```python
import functools

import jax
import jax.numpy as jnp
from jax import lax
from jax.experimental import pallas as pl
from jax.experimental.pallas import tpu as pltpu
from jax.sharding import PartitionSpec as P

BUCKETS = 32
EPS = 1e-06
NEG = -1e30
MESH = pl.DeviceIdType.MESH
CUBE = 8
VMEM_LIMIT = 56 * 1024 * 1024


def run_together(*streams):
    streams = list(streams)
    while streams:
        for stream in list(streams):
            try:
                next(stream)
            except StopIteration:
                streams.remove(stream)


def greet(pos, count, cube_me):
    barrier = pltpu.get_barrier_semaphore()
    for away in range(1, count):
        pl.semaphore_signal(
            barrier,
            inc=1,
            device_id={"tensor": lax.rem(pos + away, count)},
            device_id_type=MESH,
        )
    waits = count - 1
    if cube_me is not None:
        for flip in (1, 2, 4):
            pl.semaphore_signal(
                barrier, inc=1, device_id={"dp": cube_me ^ flip}, device_id_type=MESH
            )
        waits = waits + 3
    pl.semaphore_wait(barrier, waits)


def small_sum(pos, count, me, acc, cube_got, line_got, send, recv, line_send, line_recv):
    for slot, flip in enumerate((1, 2, 4)):
        one = pltpu.make_async_remote_copy(
            src_ref=acc,
            dst_ref=cube_got.at[slot],
            send_sem=send.at[slot],
            recv_sem=recv.at[slot],
            device_id={"dp": me ^ flip},
            device_id_type=MESH,
        )
        one.start()
        one.wait()
        acc[...] = acc[...] + cube_got[slot]
    copies = []
    for away in range(1, count):
        one = pltpu.make_async_remote_copy(
            src_ref=acc,
            dst_ref=line_got.at[away - 1],
            send_sem=line_send.at[away - 1],
            recv_sem=line_recv.at[away - 1],
            device_id={"tensor": lax.rem(pos + away, count)},
            device_id_type=MESH,
        )
        one.start()
        copies.append(one)
    for one in copies:
        one.wait()
    for away in range(1, count):
        acc[...] = acc[...] + line_got[away - 1]


def line_gather(pos, count, buf, send, recv):
    micro = buf.shape[0]
    rows = buf.shape[1] // count

    def piece(block, step):
        return buf.at[step, pl.ds(pl.multiple_of(block * rows, rows), rows)]

    def copy(block, step, target, way):
        return pltpu.make_async_remote_copy(
            src_ref=piece(block, step),
            dst_ref=piece(block, step),
            send_sem=send.at[way, block, step],
            recv_sem=recv.at[block, step],
            device_id={"tensor": target},
            device_id_type=MESH,
        )

    for hop in range(count):
        for step in range(micro):
            for way, target, block, can_send in (
                (0, pos + 1, pos - hop, pos < count - 1),
                (1, pos - 1, pos + hop, pos > 0),
            ):
                there = (block >= 0) & (block < count)

                if hop > 0:

                    @pl.when(there)
                    def _(block=block, step=step, way=way, target=target):
                        copy(block, step, target, way).wait_recv()

                if hop < count - 1:

                    @pl.when(there & can_send)
                    def _(block=block, step=step, way=way, target=target):
                        copy(block, step, target, way).start()

        yield
    for hop in range(count - 1):
        for step in range(micro):
            for way, target, block, can_send in (
                (0, pos + 1, pos - hop, pos < count - 1),
                (1, pos - 1, pos + hop, pos > 0),
            ):

                @pl.when((block >= 0) & (block < count) & can_send)
                def _(block=block, step=step, way=way, target=target):
                    copy(block, step, target, way).wait_send()


def line_scatter(pos, count, parts, got, staged, total, send, recv):
    micro = parts.shape[0]
    rows = parts.shape[1] // count

    def at(block):
        return pl.ds(pl.multiple_of(block * rows, rows), rows)

    def copy(block, step, target, way):
        return pltpu.make_async_remote_copy(
            src_ref=staged.at[way, step, at(block)],
            dst_ref=got.at[way, step, at(block)],
            send_sem=send.at[way, block, step],
            recv_sem=recv.at[way, block, step],
            device_id={"tensor": target},
            device_id_type=MESH,
        )

    def ways(hop):
        return (
            (0, pos + 1, pos + hop, pos + hop < count, pos > 0),
            (1, pos - 1, pos - hop, pos - hop >= 0, pos < count - 1),
        )

    for hop in range(count - 1, 0, -1):
        for step in range(micro):
            for way, target, block, there, has_input in ways(hop):

                @pl.when(there & has_input)
                def _(way=way, target=target, block=block, step=step):
                    copy(block, step, target, way).wait_recv()
                    staged[way, step, at(block)] = (
                        parts[step, at(block)].astype(jnp.float32)
                        + got[way, step, at(block)].astype(jnp.float32)
                    ).astype(staged.dtype)
                    copy(block, step, target, way).start()

                @pl.when(there & jnp.logical_not(has_input))
                def _(way=way, target=target, block=block, step=step):
                    staged[way, step, at(block)] = parts[step, at(block)]
                    copy(block, step, target, way).start()

        yield
    for step in range(micro):
        total[step] = parts[step, at(pos)].astype(jnp.float32)
        for way, target, block, there, has_input in ways(0):

            @pl.when(has_input)
            def _(way=way, target=target, step=step):
                copy(pos, step, target, way).wait_recv()
                total[step] = total[step] + got[way, step, at(pos)].astype(jnp.float32)

    for hop in range(count - 1, 0, -1):
        for step in range(micro):
            for way, target, block, there, has_input in ways(hop):

                @pl.when(there)
                def _(way=way, target=target, block=block, step=step):
                    copy(block, step, target, way).wait_send()


def cube_gather(me, buf, send, recv):
    half_rows = buf.shape[1] // 2

    def copy(block, half, flip, slot):
        piece = buf.at[block, pl.ds(half * half_rows, half_rows)]
        return pltpu.make_async_remote_copy(
            src_ref=piece,
            dst_ref=piece,
            send_sem=send.at[slot, half],
            recv_sem=recv.at[block, half],
            device_id={"dp": me ^ flip},
            device_id_type=MESH,
        )

    started = []

    def begin(block, half, flip):
        one = copy(block, half, flip, len(started) // 2 if half == 0 else len(started) // 2)
        one.start()
        started.append(one)

    firsts = ((2, 4), (4, 2))
    for half in range(2):
        begin(me, half, firsts[half][0])
    for half in range(2):
        begin(me, half, firsts[half][1])
    for half in range(2):
        begin(me, half, 1)
    yield
    for half in range(2):
        first, second = firsts[half]
        copy(me ^ first, half, first, 0).wait_recv()
        begin(me ^ first, half, second)
    for half in range(2):
        begin(me ^ firsts[half][0], half, 1)
    yield
    for half in range(2):
        copy(me ^ firsts[half][1], half, firsts[half][1], 0).wait_recv()
        begin(me ^ firsts[half][1], half, 1)
    yield
    for half in range(2):
        copy(me ^ 6, half, firsts[half][1], 0).wait_recv()
        begin(me ^ 6, half, 1)
    yield
    for other in (0, 2, 4, 6):
        for half in range(2):
            copy(me ^ 1 ^ other, half, 1, 0).wait_recv()
    for one in started:
        one.wait_send()


def cube_scatter(me, parts, got1, sums, got2, got3, total, send1, recv1, send2, recv2, send3, recv3):
    half_rows = parts.shape[1] // 2
    firsts = ((2, 4), (4, 2))

    def rows_of(half):
        return pl.ds(half * half_rows, half_rows)

    def one_copy(src, dst, send, recv, flip):
        return pltpu.make_async_remote_copy(
            src_ref=src,
            dst_ref=dst,
            send_sem=send,
            recv_sem=recv,
            device_id={"dp": me ^ flip},
            device_id_type=MESH,
        )

    first_copies = {}
    for slot in (3, 1, 2, 0):
        first_copies[slot] = one_copy(
            parts.at[me ^ 1 ^ (2 * slot)], got1.at[slot], send1.at[slot], recv1.at[slot], 1
        )
        first_copies[slot].start()
    yield
    second_copies = {}
    for slot in (3, 1, 2, 0):
        first_copies[slot].wait_recv()
        sums[slot] = (
            parts[me ^ (2 * slot)].astype(jnp.float32) + got1[slot].astype(jnp.float32)
        ).astype(sums.dtype)
        for half in range(2):
            first, second = firsts[half]
            if slot == 3 or slot == first // 2:
                goes = 1 if slot == 3 else 0
                second_copies[half, goes] = one_copy(
                    sums.at[slot, rows_of(half)],
                    got2.at[half, goes],
                    send2.at[half, goes],
                    recv2.at[half, goes],
                    first,
                )
                second_copies[half, goes].start()
    yield
    third_copies = {}
    for half in range(2):
        first, second = firsts[half]
        second_copies[half, 1].wait_recv()
        slot = second // 2
        sums[slot, rows_of(half)] = (
            sums[slot, rows_of(half)].astype(jnp.float32) + got2[half, 1].astype(jnp.float32)
        ).astype(sums.dtype)
        third_copies[half] = one_copy(
            sums.at[slot, rows_of(half)], got3.at[half], send3.at[half], recv3.at[half], second
        )
        third_copies[half].start()
    yield
    for half in range(2):
        second_copies[half, 0].wait_recv()
        total[rows_of(half)] = sums[0, rows_of(half)].astype(jnp.float32) + got2[half, 0].astype(
            jnp.float32
        )
    yield
    for half in range(2):
        third_copies[half].wait_recv()
        total[rows_of(half)] = total[rows_of(half)] + got3[half].astype(jnp.float32)
    for group in (first_copies, second_copies, third_copies):
        for one in group.values():
            one.wait_send()


def norm_forward(values, gain_row):
    inv_root = lax.rsqrt(jnp.mean(values * values, axis=-1, keepdims=True) + EPS)
    return values * inv_root * gain_row


def norm_backward(grad_out, values, gain_row):
    inv_root = lax.rsqrt(jnp.mean(values * values, axis=-1, keepdims=True) + EPS)
    normal = values * inv_root
    scaled = grad_out * gain_row
    values_grad = inv_root * (scaled - normal * jnp.mean(scaled * normal, axis=-1, keepdims=True))
    return (values_grad, jnp.sum(grad_out * normal, axis=0, keepdims=True))


def own_rows(pos, buf, count):
    rows = buf.shape[1] // count
    return pl.ds(pl.multiple_of(pos * rows, rows), rows)


def scatter_scratch(shape):
    return [
        pltpu.VMEM((2,) + shape, jnp.bfloat16),
        pltpu.VMEM((2,) + shape, jnp.bfloat16),
    ]


def scatter_sems(count, micro):
    return [
        pltpu.SemaphoreType.DMA((2, count, micro)),
        pltpu.SemaphoreType.DMA((2, count, micro)),
    ]


def gather_sems(count, micro):
    return [
        pltpu.SemaphoreType.DMA((2, count, micro)),
        pltpu.SemaphoreType.DMA((count, micro)),
    ]


def call(kernel, outs, scratch, ident, name, *args):
    return pl.pallas_call(
        kernel,
        out_shape=[jax.ShapeDtypeStruct(shape, kind) for shape, kind in outs],
        in_specs=[pl.BlockSpec(memory_space=pltpu.VMEM)] * len(args),
        out_specs=[pl.BlockSpec(memory_space=pltpu.VMEM)] * len(outs),
        scratch_shapes=scratch,
        compiler_params=pltpu.CompilerParams(
            collective_id=ident, has_side_effects=True, vmem_limit_bytes=VMEM_LIMIT
        ),
        name=name,
    )(*args)


def entry_kernel(count, with_cube, *refs):
    if with_cube:
        weights, refs = refs[0], refs[1:]
    rows_in, refs = refs[:2], refs[2:]
    if with_cube:
        weights_all, refs = refs[0], refs[1:]
    rows_out, refs = refs[:2], refs[2:]
    pos = lax.axis_index("tensor")
    me = lax.axis_index("dp") if with_cube else None
    for source, target in zip(rows_in, rows_out):
        for step in range(source.shape[0]):
            target[step, own_rows(pos, target, count)] = source[step]
    if with_cube:
        weights_all[me] = weights[...]
    greet(pos, count, me)
    streams = []
    if with_cube:
        streams.append(cube_gather(me, weights_all, refs[4], refs[5]))
    for which in range(2):
        streams.append(
            line_gather(pos, count, rows_out[which], refs[2 * which], refs[2 * which + 1])
        )
    run_together(*streams)


def forward_kernel(count, beside, *refs):
    parts, resid, gain = refs[:3]
    refs = refs[3:]
    if beside:
        extra, refs = refs[0], refs[1:]
    total_out, normed_all = refs[:2]
    refs = refs[2:]
    if beside:
        extra_all, refs = refs[0], refs[1:]
    got, staged, s_send, s_recv, g_send, g_recv = refs[:6]
    pos = lax.axis_index("tensor")
    me = lax.axis_index("dp") if beside == "cube" else None
    streams = []
    if beside == "cube":
        extra_all[me] = extra[...]
    if beside == "line":
        for step in range(extra.shape[0]):
            extra_all[step, own_rows(pos, extra_all, count)] = extra[step]
    greet(pos, count, me)

    def main():
        yield from line_scatter(pos, count, parts, got, staged, total_out, s_send, s_recv)
        for step in range(parts.shape[0]):
            total = total_out[step] + resid[step].astype(jnp.float32)
            total_out[step] = total
            normed_all[step, own_rows(pos, normed_all, count)] = norm_forward(
                total, gain[...]
            ).astype(jnp.bfloat16)
        yield from line_gather(pos, count, normed_all, g_send, g_recv)

    streams.append(main())
    if beside == "cube":
        streams.append(cube_gather(me, extra_all, refs[6], refs[7]))
    if beside == "line":
        streams.append(line_gather(pos, count, extra_all, refs[6], refs[7]))
    run_together(*streams)


def back_kernel(count, side_kind, cubes, *refs):
    parts, side_parts, values, gain, grad_in, side_resid = refs[:6]
    refs = refs[6:]
    weight_parts, refs = refs[:cubes], refs[cubes:]
    grad_out, gathered, side_out, gain_out = refs[:4]
    refs = refs[4:]
    weight_out, refs = refs[:cubes], refs[cubes:]
    got, staged, side_got, side_staged, side_total = refs[:5]
    s_send, s_recv, t_send, t_recv, g_send, g_recv = refs[5:11]
    refs = refs[11:]
    pos = lax.axis_index("tensor")
    me = lax.axis_index("dp") if cubes else None
    greet(pos, count, me)

    def main():
        yield from line_scatter(pos, count, parts, got, staged, grad_out, s_send, s_recv)
        gain_out[...] = jnp.zeros_like(gain_out)
        for step in range(parts.shape[0]):
            moved, gain_part = norm_backward(grad_out[step], values[step], gain[...])
            total = grad_in[step].astype(jnp.float32) + moved
            grad_out[step] = total
            gain_out[...] = gain_out[...] + gain_part
            gathered[step, own_rows(pos, gathered, count)] = total.astype(jnp.bfloat16)
        yield from line_gather(pos, count, gathered, g_send, g_recv)

    def side():
        yield from line_scatter(
            pos, count, side_parts, side_got, side_staged, side_total, t_send, t_recv
        )
        for step in range(parts.shape[0]):
            if side_kind == "out":
                side_out[step] = (side_total[step] + side_resid[step]).astype(jnp.bfloat16)
            else:
                side_out[step] = side_total[step]

    run_together(main(), side(), *cube_streams(me, weight_parts, weight_out, refs))


def cube_streams(me, weight_parts, weight_out, refs):
    return [
        cube_scatter(
            me,
            weight_parts[which],
            *refs[10 * which : 10 * which + 4],
            weight_out[which],
            *refs[10 * which + 4 : 10 * which + 10],
        )
        for which in range(len(weight_parts))
    ]


def cube_scratch(shard_rows, columns):
    return [
        pltpu.VMEM((4, shard_rows, columns), jnp.bfloat16),
        pltpu.VMEM((4, shard_rows, columns), jnp.bfloat16),
        pltpu.VMEM((2, 2, shard_rows // 2, columns), jnp.bfloat16),
        pltpu.VMEM((2, shard_rows // 2, columns), jnp.bfloat16),
        pltpu.SemaphoreType.DMA((4,)),
        pltpu.SemaphoreType.DMA((4,)),
        pltpu.SemaphoreType.DMA((2, 2)),
        pltpu.SemaphoreType.DMA((2, 2)),
        pltpu.SemaphoreType.DMA((2,)),
        pltpu.SemaphoreType.DMA((2,)),
    ]


def exit_kernel(count, cubes, *refs):
    parts, values, gain, grad_in, small = refs[:5]
    refs = refs[5:]
    weight_parts, refs = refs[:cubes], refs[cubes:]
    grad_out, small_out = refs[:2]
    refs = refs[2:]
    weight_out, refs = refs[:cubes], refs[cubes:]
    got, staged, s_send, s_recv = refs[:4]
    refs = refs[4:]
    pos = lax.axis_index("tensor")
    me = lax.axis_index("dp") if cubes else None
    greet(pos, count, me)

    def main():
        yield from line_scatter(pos, count, parts, got, staged, grad_out, s_send, s_recv)
        small_out[...] = small[...]
        for step in range(parts.shape[0]):
            moved, gain_part = norm_backward(
                grad_out[step], values[step].astype(jnp.float32), gain[...]
            )
            grad_out[step] = grad_in[step] + moved
            small_out[0:1] = small_out[0:1] + gain_part

    run_together(main(), *cube_streams(me, weight_parts, weight_out, refs))
    if cubes:
        small_sum(pos, count, me, small_out, *refs[10 * cubes :])


def dot_plain(left, right):
    return jnp.dot(left, right, preferred_element_type=jnp.float32)


def dot_left_t(left, right):
    return lax.dot_general(
        left, right, (((0,), (0,)), ((), ())), preferred_element_type=jnp.float32
    )


def dot_right_t(left, right):
    return lax.dot_general(
        left, right, (((1,), (1,)), ((), ())), preferred_element_type=jnp.float32
    )


def gelu_tanh(values):
    return jax.nn.gelu(values, approximate=True)


def head_split(values, heads_local):
    return values.reshape(values.shape[:2] + (heads_local, values.shape[2] // heads_local))


def attend_forward(query_rows, key_rows, value_rows, heads_local, extra, allowed):
    scores = (
        jnp.einsum(
            "bqhd,bkhd->bhqk",
            head_split(query_rows, heads_local),
            head_split(key_rows, heads_local),
            preferred_element_type=jnp.float32,
        )
        + extra
    )
    scores = jnp.where(allowed[:, None], scores, NEG)
    biggest = jnp.max(scores, axis=-1, keepdims=True)
    exponent = jnp.exp(scores - biggest)
    probs = exponent / jnp.sum(exponent, axis=-1, keepdims=True)
    mixed = jnp.einsum(
        "bhqk,bkhd->bqhd",
        probs.astype(jnp.bfloat16),
        head_split(value_rows, heads_local),
        preferred_element_type=jnp.float32,
    )
    return (mixed.reshape(query_rows.shape).astype(jnp.bfloat16), probs)


def attend_backward(query_rows, key_rows, value_rows, heads_local, probs, mixed_grad):
    grad_heads = head_split(mixed_grad, heads_local)
    query_heads = head_split(query_rows, heads_local)
    key_heads = head_split(key_rows, heads_local)
    prob_grad = jnp.einsum(
        "bqhd,bkhd->bhqk",
        grad_heads,
        head_split(value_rows, heads_local),
        preferred_element_type=jnp.float32,
    )
    score_low = (probs * (prob_grad - jnp.sum(probs * prob_grad, axis=-1, keepdims=True))).astype(
        jnp.bfloat16
    )
    query_grad = jnp.einsum(
        "bhqk,bkhd->bqhd", score_low, key_heads, preferred_element_type=jnp.float32
    )
    key_grad = jnp.einsum(
        "bhqk,bqhd->bkhd", score_low, query_heads, preferred_element_type=jnp.float32
    )
    value_grad = jnp.einsum(
        "bhqk,bqhd->bkhd", probs.astype(jnp.bfloat16), grad_heads, preferred_element_type=jnp.float32
    )
    return (
        query_grad.reshape(query_rows.shape).astype(jnp.bfloat16),
        key_grad.reshape(key_rows.shape).astype(jnp.bfloat16),
        value_grad.reshape(key_rows.shape).astype(jnp.bfloat16),
        score_low,
    )


def rows_dot(rows, matrix):
    return lax.dot_general(
        rows, matrix, (((2,), (0,)), ((), ())), preferred_element_type=jnp.float32
    )


def rows_dot_t(rows, matrix):
    return lax.dot_general(
        rows, matrix, (((2,), (1,)), ((), ())), preferred_element_type=jnp.float32
    )


def weight_dot(left, right):
    return dot_left_t(
        left.reshape(-1, left.shape[-1]), right.reshape(-1, right.shape[-1])
    ).astype(jnp.bfloat16)

def bias_kernel(rows, out):
    length = out.shape[1]
    for head in range(out.shape[0]):
        out[head] = pltpu.roll(
            jnp.broadcast_to(rows[head : head + 1], (length, length)), 0, 1, stride=1, stride_axis=0
        )


def diagonal_kernel(scores, out):
    length = scores.shape[2]
    turned = (
        lax.broadcasted_iota(jnp.int32, (length, length), 0)
        + lax.broadcasted_iota(jnp.int32, (length, length), 1)
        == length - 1
    ).astype(jnp.bfloat16)
    for head in range(scores.shape[1]):
        flipped = jnp.dot(turned, scores[0, head], preferred_element_type=jnp.float32)
        for step in range(1, scores.shape[0]):
            flipped = flipped + jnp.dot(
                turned, scores[step, head], preferred_element_type=jnp.float32
            )
        moved = pltpu.roll(flipped, 1, 1, stride=1, stride_axis=0)
        out[head : head + 1] = jnp.sum(moved, axis=0, keepdims=True)


def local_call(kernel, shape, name, arg):
    return pl.pallas_call(
        kernel,
        out_shape=jax.ShapeDtypeStruct(shape, jnp.float32),
        in_specs=[pl.BlockSpec(memory_space=pltpu.VMEM)],
        out_specs=pl.BlockSpec(memory_space=pltpu.VMEM),
        compiler_params=pltpu.CompilerParams(vmem_limit_bytes=VMEM_LIMIT),
        name=name,
    )(arg)


def body(
    tokens,
    encoder,
    cotangent,
    dec_segments,
    enc_segments,
    buckets,
    self_query,
    self_key,
    self_value,
    self_output,
    cross_query,
    cross_key,
    cross_value,
    cross_output,
    gate_weight,
    up_weight,
    down_weight,
    gain_self,
    gain_cross,
    gain_feed,
    bias_table,
):
    low = jnp.bfloat16
    dp_count = lax.axis_size("dp")
    count = lax.axis_size("tensor")
    heads_local = bias_table.shape[1]
    inner = self_query.shape[1]
    hidden_local = gate_weight.shape[1]
    shard_rows = self_query.shape[0]
    width = shard_rows * dp_count
    micro, row_count = tokens.shape[:2]
    seq_len = row_count * count
    enc_len = encoder.shape[1] * count
    with_cube = dp_count == CUBE and shard_rows % 32 == 0

    gain_columns = jnp.pad(
        jnp.stack([gain_self, gain_cross, gain_feed], axis=1), ((0, 0), (0, 125))
    )
    packed = jnp.concatenate(
        [
            self_query,
            self_key,
            self_value,
            cross_query,
            cross_key,
            cross_value,
            self_output.T,
            cross_output.T,
            gain_columns,
        ],
        axis=1,
    )
    packed_feed = jnp.concatenate([gate_weight, up_weight, down_weight.T], axis=1)
    cube_sems = [pltpu.SemaphoreType.DMA((8, 2)), pltpu.SemaphoreType.DMA((CUBE, 2))]
    rows_shape = (micro, seq_len, width)
    enc_shape = (micro, enc_len, width)
    own_shape = (micro, row_count, width)
    line_sems = gather_sems(count, micro)
    entry_args = [tokens, encoder]
    entry_outs = [(rows_shape, low), (enc_shape, low)]
    entry_scratch = line_sems * 2
    if with_cube:
        entry_args.insert(0, packed)
        entry_outs.insert(0, ((CUBE,) + packed.shape, low))
        entry_scratch = entry_scratch + cube_sems
    entry = call(
        functools.partial(entry_kernel, count, with_cube),
        entry_outs,
        entry_scratch,
        0,
        "entry_gather",
        *entry_args,
    )
    if with_cube:
        whole, tokens_all, encoder_all = entry
        whole = whole.reshape(width, packed.shape[1])
    else:
        tokens_all, encoder_all = entry
        whole = lax.all_gather(packed, "dp", axis=0, tiled=True)
    base = 0
    w_qkv = whole[:, base : base + 3 * inner]
    w_cq = whole[:, base + 3 * inner : base + 4 * inner]
    w_ckv = whole[:, base + 4 * inner : base + 6 * inner]
    w_so_t = whole[:, base + 6 * inner : base + 7 * inner]
    w_co_t = whole[:, base + 7 * inner : base + 8 * inner]
    gains = whole[:, base + 8 * inner : base + 8 * inner + 3].T.astype(jnp.float32)
    gain1, gain2, gain3 = gains[0:1], gains[1:2], gains[2:3]

    position = jnp.arange(seq_len, dtype=jnp.int32)
    causal = position[:, None] >= position[None, :]
    buckets_back = jnp.concatenate([buckets[:1], buckets[1:][::-1]])
    hits_back = buckets_back[:, None] == jnp.arange(BUCKETS, dtype=jnp.int32)[None, :]
    bias_rows = lax.dot_general(
        bias_table, hits_back.astype(low), (((0,), (1,)), ((), ())), preferred_element_type=jnp.float32
    )
    bias_full = local_call(
        bias_kernel, (heads_local, seq_len, seq_len), "bias_spread", bias_rows
    )
    dec_seg = dec_segments[:, 0]
    enc_seg = enc_segments[:, 0]
    self_allowed = causal[None] & (dec_seg[:, :, None] == dec_seg[:, None, :])
    cross_allowed = dec_seg[:, :, None] == enc_seg[:, None, :]

    forward_scratch = (
        scatter_scratch(rows_shape) + scatter_sems(count, micro) + gather_sems(count, micro)
    )
    normed1_all = norm_forward(tokens_all.astype(jnp.float32), gain1).astype(low)
    qkv = rows_dot(normed1_all, w_qkv).astype(low)
    query1, key1, value1 = (
        qkv[..., :inner],
        qkv[..., inner : 2 * inner],
        qkv[..., 2 * inner :],
    )
    mixed1, probs1 = attend_forward(query1, key1, value1, heads_local, bias_full, self_allowed)
    self_args = [rows_dot_t(mixed1, w_so_t).astype(low), tokens, gain2]
    self_outs = [(own_shape, jnp.float32), (rows_shape, low)]
    if with_cube:
        self_args.append(packed_feed)
        self_outs.append(((CUBE,) + packed_feed.shape, low))
    self_ended = call(
        functools.partial(forward_kernel, count, "cube" if with_cube else ""),
        self_outs,
        forward_scratch + (cube_sems if with_cube else []),
        1,
        "self_sum_norm",
        *self_args,
    )
    if with_cube:
        first, normed2_all, feed_whole = self_ended
        feed_whole = feed_whole.reshape(width, packed_feed.shape[1])
    else:
        first, normed2_all = self_ended
        feed_whole = lax.all_gather(packed_feed, "dp", axis=0, tiled=True)
    w_gate_up = feed_whole[:, : 2 * hidden_local]
    w_down_t = feed_whole[:, 2 * hidden_local :]
    key_value2 = rows_dot(encoder_all, w_ckv).astype(low)
    key2, value2 = key_value2[..., :inner], key_value2[..., inner:]
    query2 = rows_dot(normed2_all, w_cq).astype(low)
    mixed2, probs2 = attend_forward(query2, key2, value2, heads_local, 0.0, cross_allowed)
    second, normed3_all, cot_all = call(
        functools.partial(forward_kernel, count, "line"),
        [(own_shape, jnp.float32), (rows_shape, low), (rows_shape, low)],
        forward_scratch + gather_sems(count, micro),
        2,
        "cross_sum_norm",
        rows_dot_t(mixed2, w_co_t).astype(low),
        first,
        gain3,
        cotangent,
    )
    gate_up = rows_dot(normed3_all, w_gate_up)
    gate_pre, up_pre = gate_up[..., :hidden_local], gate_up[..., hidden_local:]
    gate_act, gate_pull = jax.vjp(gelu_tanh, gate_pre)
    hidden = (gate_act * up_pre).astype(low)
    hidden_grad = rows_dot(cot_all, w_down_t)
    gate_grad = gate_pull(hidden_grad * up_pre)[0].astype(low)
    up_grad = (hidden_grad * gate_act).astype(low)
    gate_up_grad = jnp.concatenate([gate_grad, up_grad], axis=-1)

    def back_scratch(side_shape, side_own):
        return (
            scatter_scratch(rows_shape)
            + scatter_scratch(side_shape)
            + [pltpu.VMEM(side_own, jnp.float32)]
            + scatter_sems(count, micro) * 2
            + gather_sems(count, micro)
        )

    second_grad, cross_out_all, layer_out, gain3_part = call(
        functools.partial(back_kernel, count, "out", 0),
        [
            (own_shape, jnp.float32),
            (rows_shape, low),
            (own_shape, low),
            ((1, width), jnp.float32),
        ],
        back_scratch(rows_shape, own_shape),
        3,
        "feed_back",
        rows_dot_t(gate_up_grad, w_gate_up).astype(low),
        rows_dot_t(hidden, w_down_t).astype(low),
        second,
        gain3,
        cotangent,
        second,
    )
    mixed2_grad = rows_dot(cross_out_all, w_co_t).astype(low)
    query2_grad, key2_grad, value2_grad, score2_low = attend_backward(
        query2, key2, value2, heads_local, probs2, mixed2_grad
    )
    key_value2_grad = jnp.concatenate([key2_grad, value2_grad], axis=-1)
    enc_own = (micro, encoder.shape[1], width)
    feed_parts = [
        weight_dot(normed3_all, gate_up_grad),
        weight_dot(cot_all, hidden),
    ]

    def cube_args(parts):
        return [one.reshape(CUBE, shard_rows, one.shape[1]) for one in parts] if with_cube else []

    def cube_outs(parts):
        return [((shard_rows, one.shape[1]), jnp.float32) for one in parts] if with_cube else []

    def cube_space(parts):
        scratch = []
        if with_cube:
            for one in parts:
                scratch = scratch + cube_scratch(shard_rows, one.shape[1])
        return scratch

    def owned_parts(ended, parts):
        if with_cube:
            return ended
        return [
            lax.psum_scatter(one.astype(jnp.float32), "dp", scatter_dimension=0, tiled=True)
            for one in parts
        ]

    first_grad, self_out_all, encoder_grad, gain2_part, *feed_ended = call(
        functools.partial(back_kernel, count, "plain", len(cube_args(feed_parts))),
        [
            (own_shape, jnp.float32),
            (rows_shape, low),
            (enc_own, jnp.float32),
            ((1, width), jnp.float32),
        ]
        + cube_outs(feed_parts),
        back_scratch(enc_shape, enc_own) + cube_space(feed_parts),
        4,
        "cross_back",
        rows_dot_t(query2_grad, w_cq).astype(low),
        rows_dot_t(key_value2_grad, w_ckv).astype(low),
        first,
        gain2,
        second_grad,
        second,
        *cube_args(feed_parts),
    )
    mixed1_grad = rows_dot(self_out_all, w_so_t).astype(low)
    query1_grad, key1_grad, value1_grad, score1_low = attend_backward(
        query1, key1, value1, heads_local, probs1, mixed1_grad
    )
    qkv_grad = jnp.concatenate([query1_grad, key1_grad, value1_grad], axis=-1)
    head_parts = [
        weight_dot(normed1_all, qkv_grad),
        jnp.concatenate(
            [
                weight_dot(normed2_all, query2_grad),
                weight_dot(encoder_all, key_value2_grad),
                weight_dot(self_out_all, mixed1),
                weight_dot(cross_out_all, mixed2),
            ],
            axis=1,
        ),
    ]
    per_distance = local_call(
        diagonal_kernel, (heads_local, seq_len), "diagonal_sums", score1_low
    )
    tables = lax.dot_general(
        hits_back.astype(jnp.float32),
        per_distance,
        (((0,), (1,)), ((), ())),
        precision=lax.Precision.HIGHEST,
        preferred_element_type=jnp.float32,
    )
    pos = lax.axis_index("tensor")
    table_size = tables.shape[0] * tables.shape[1]
    placed_table = jnp.where(
        (jnp.arange(count, dtype=jnp.int32) == pos)[:, None], tables.reshape(1, -1), 0.0
    ).reshape(1, -1)
    small = jnp.concatenate(
        [
            jnp.zeros((1, width), jnp.float32),
            gain2_part,
            gain3_part,
            jnp.pad(placed_table, ((0, 0), (0, width - count * table_size))),
            jnp.zeros((4, width), jnp.float32),
        ],
        axis=0,
    )
    exit_scratch = (
        scatter_scratch(rows_shape) + scatter_sems(count, micro) + cube_space(head_parts)
    )
    if with_cube:
        exit_scratch = exit_scratch + [
            pltpu.VMEM((3,) + small.shape, jnp.float32),
            pltpu.VMEM((count - 1,) + small.shape, jnp.float32),
            pltpu.SemaphoreType.DMA((3,)),
            pltpu.SemaphoreType.DMA((3,)),
            pltpu.SemaphoreType.DMA((count - 1,)),
            pltpu.SemaphoreType.DMA((count - 1,)),
        ]
    token_grad, small_out, *head_ended = call(
        functools.partial(exit_kernel, count, len(cube_args(head_parts))),
        [(own_shape, jnp.float32), (small.shape, jnp.float32)] + cube_outs(head_parts),
        exit_scratch,
        5,
        "exit_sums",
        rows_dot_t(qkv_grad, w_qkv).astype(low),
        tokens,
        gain1,
        first_grad,
        small,
        *cube_args(head_parts),
    )
    if not with_cube:
        small_out = lax.psum(small_out, ("dp", "tensor"))
    gate_up_owned, down_owned = owned_parts(feed_ended, feed_parts)
    qkv_owned, others = owned_parts(head_ended, head_parts)
    index = lax.axis_index("dp") * count + pos
    piece = width // (dp_count * count)
    gain_grads = tuple(
        lax.dynamic_slice(small_out, (which, index * piece), (1, piece)).reshape(-1)
        for which in range(3)
    )
    table_grad = lax.dynamic_slice(small_out, (3, pos * table_size), (1, table_size)).reshape(
        tables.shape
    )

    return (
        layer_out,
        token_grad,
        encoder_grad,
        qkv_owned[:, :inner],
        qkv_owned[:, inner : 2 * inner],
        qkv_owned[:, 2 * inner :],
        others[:, 3 * inner : 4 * inner].T,
        others[:, :inner],
        others[:, inner : 2 * inner],
        others[:, 2 * inner : 3 * inner],
        others[:, 4 * inner :].T,
        gate_up_owned[:, :hidden_local],
        gate_up_owned[:, hidden_local:],
        down_owned.T,
    ) + gain_grads + (table_grad,)


def solution(mesh):
    placed = (
        P(None, ("dp", "tensor"), None),
        P(None, ("dp", "tensor"), None),
        P(None, ("dp", "tensor"), None),
        P(None, "dp", None),
        P(None, "dp", None),
        P(),
        P("dp", "tensor"),
        P("dp", "tensor"),
        P("dp", "tensor"),
        P("tensor", "dp"),
        P("dp", "tensor"),
        P("dp", "tensor"),
        P("dp", "tensor"),
        P("tensor", "dp"),
        P("dp", "tensor"),
        P("dp", "tensor"),
        P("tensor", "dp"),
        P("dp"),
        P("dp"),
        P("dp"),
        P(None, "tensor"),
    )
    return jax.shard_map(
        body,
        mesh=mesh,
        in_specs=placed,
        out_specs=(
            P(None, ("dp", "tensor"), None),
            P(None, ("dp", "tensor"), None),
            P(None, ("dp", "tensor"), None),
            P("dp", "tensor"),
            P("dp", "tensor"),
            P("dp", "tensor"),
            P("tensor", "dp"),
            P("dp", "tensor"),
            P("dp", "tensor"),
            P("dp", "tensor"),
            P("tensor", "dp"),
            P("dp", "tensor"),
            P("dp", "tensor"),
            P("tensor", "dp"),
            P(("dp", "tensor")),
            P(("dp", "tensor")),
            P(("dp", "tensor")),
            P(None, "tensor"),
        ),
        check_vma=False,
    )
```

```python
import functools

import jax
import jax.numpy as jnp
from jax import lax
from jax.experimental import pallas as pl
from jax.experimental.pallas import tpu as pltpu
from jax.sharding import PartitionSpec as P

BUCKETS = 32
EPS = 1e-06
NEG = -1e30
MESH = pl.DeviceIdType.MESH
CUBE = 8
VMEM_LIMIT = 56 * 1024 * 1024


def run_together(*streams):
    streams = list(streams)
    while streams:
        for stream in list(streams):
            try:
                next(stream)
            except StopIteration:
                streams.remove(stream)


def greet(pos, count, cube_me):
    barrier = pltpu.get_barrier_semaphore()
    for away in range(1, count):
        pl.semaphore_signal(
            barrier,
            inc=1,
            device_id={"tensor": lax.rem(pos + away, count)},
            device_id_type=MESH,
        )
    waits = count - 1
    if cube_me is not None:
        for flip in (1, 2, 4):
            pl.semaphore_signal(
                barrier, inc=1, device_id={"dp": cube_me ^ flip}, device_id_type=MESH
            )
        waits = waits + 3
    pl.semaphore_wait(barrier, waits)


def small_sum(pos, count, me, acc, cube_got, line_got, send, recv, line_send, line_recv):
    for slot, flip in enumerate((1, 2, 4)):
        one = pltpu.make_async_remote_copy(
            src_ref=acc,
            dst_ref=cube_got.at[slot],
            send_sem=send.at[slot],
            recv_sem=recv.at[slot],
            device_id={"dp": me ^ flip},
            device_id_type=MESH,
        )
        one.start()
        one.wait()
        acc[...] = acc[...] + cube_got[slot]
    copies = []
    for away in range(1, count):
        one = pltpu.make_async_remote_copy(
            src_ref=acc,
            dst_ref=line_got.at[away - 1],
            send_sem=line_send.at[away - 1],
            recv_sem=line_recv.at[away - 1],
            device_id={"tensor": lax.rem(pos + away, count)},
            device_id_type=MESH,
        )
        one.start()
        copies.append(one)
    for one in copies:
        one.wait()
    for away in range(1, count):
        acc[...] = acc[...] + line_got[away - 1]


def line_gather(pos, count, buf, send, recv, steps=None):
    steps = range(buf.shape[0]) if steps is None else steps
    rows = buf.shape[1] // count

    def piece(block, step):
        return buf.at[step, pl.ds(pl.multiple_of(block * rows, rows), rows)]

    def copy(block, step, target, way):
        return pltpu.make_async_remote_copy(
            src_ref=piece(block, step),
            dst_ref=piece(block, step),
            send_sem=send.at[way, block, step],
            recv_sem=recv.at[block, step],
            device_id={"tensor": target},
            device_id_type=MESH,
        )

    for hop in range(count):
        for step in steps:
            for way, target, block, can_send in (
                (0, pos + 1, pos - hop, pos < count - 1),
                (1, pos - 1, pos + hop, pos > 0),
            ):
                there = (block >= 0) & (block < count)

                if hop > 0:

                    @pl.when(there)
                    def _(block=block, step=step, way=way, target=target):
                        copy(block, step, target, way).wait_recv()

                if hop < count - 1:

                    @pl.when(there & can_send)
                    def _(block=block, step=step, way=way, target=target):
                        copy(block, step, target, way).start()

        yield
    for hop in range(count - 1):
        for step in steps:
            for way, target, block, can_send in (
                (0, pos + 1, pos - hop, pos < count - 1),
                (1, pos - 1, pos + hop, pos > 0),
            ):

                @pl.when((block >= 0) & (block < count) & can_send)
                def _(block=block, step=step, way=way, target=target):
                    copy(block, step, target, way).wait_send()


def line_scatter(pos, count, parts, got, staged, total, send, recv, steps=None):
    steps = range(parts.shape[0]) if steps is None else steps
    rows = parts.shape[1] // count

    def at(block):
        return pl.ds(pl.multiple_of(block * rows, rows), rows)

    def copy(block, step, target, way):
        return pltpu.make_async_remote_copy(
            src_ref=staged.at[way, step, at(block)],
            dst_ref=got.at[way, step, at(block)],
            send_sem=send.at[way, block, step],
            recv_sem=recv.at[way, block, step],
            device_id={"tensor": target},
            device_id_type=MESH,
        )

    def ways(hop):
        return (
            (0, pos + 1, pos + hop, pos + hop < count, pos > 0),
            (1, pos - 1, pos - hop, pos - hop >= 0, pos < count - 1),
        )

    for hop in range(count - 1, 0, -1):
        for step in steps:
            for way, target, block, there, has_input in ways(hop):

                @pl.when(there & has_input)
                def _(way=way, target=target, block=block, step=step):
                    copy(block, step, target, way).wait_recv()
                    staged[way, step, at(block)] = (
                        parts[step, at(block)].astype(jnp.float32)
                        + got[way, step, at(block)].astype(jnp.float32)
                    ).astype(staged.dtype)
                    copy(block, step, target, way).start()

                @pl.when(there & jnp.logical_not(has_input))
                def _(way=way, target=target, block=block, step=step):
                    staged[way, step, at(block)] = parts[step, at(block)]
                    copy(block, step, target, way).start()

        yield
    for step in steps:
        total[step] = parts[step, at(pos)].astype(jnp.float32)
        for way, target, block, there, has_input in ways(0):

            @pl.when(has_input)
            def _(way=way, target=target, step=step):
                copy(pos, step, target, way).wait_recv()
                total[step] = total[step] + got[way, step, at(pos)].astype(jnp.float32)

    for hop in range(count - 1, 0, -1):
        for step in steps:
            for way, target, block, there, has_input in ways(hop):

                @pl.when(there)
                def _(way=way, target=target, block=block, step=step):
                    copy(block, step, target, way).wait_send()


def cube_gather(me, buf, send, recv):
    half_rows = buf.shape[1] // 2

    def copy(block, half, flip, slot):
        piece = buf.at[block, pl.ds(half * half_rows, half_rows)]
        return pltpu.make_async_remote_copy(
            src_ref=piece,
            dst_ref=piece,
            send_sem=send.at[slot, half],
            recv_sem=recv.at[block, half],
            device_id={"dp": me ^ flip},
            device_id_type=MESH,
        )

    started = []

    def begin(block, half, flip):
        one = copy(block, half, flip, len(started) // 2 if half == 0 else len(started) // 2)
        one.start()
        started.append(one)

    firsts = ((2, 4), (4, 2))
    for half in range(2):
        begin(me, half, firsts[half][0])
    for half in range(2):
        begin(me, half, firsts[half][1])
    for half in range(2):
        begin(me, half, 1)
    yield
    for half in range(2):
        first, second = firsts[half]
        copy(me ^ first, half, first, 0).wait_recv()
        begin(me ^ first, half, second)
    for half in range(2):
        begin(me ^ firsts[half][0], half, 1)
    yield
    for half in range(2):
        copy(me ^ firsts[half][1], half, firsts[half][1], 0).wait_recv()
        begin(me ^ firsts[half][1], half, 1)
    yield
    for half in range(2):
        copy(me ^ 6, half, firsts[half][1], 0).wait_recv()
        begin(me ^ 6, half, 1)
    yield
    for other in (0, 2, 4, 6):
        for half in range(2):
            copy(me ^ 1 ^ other, half, 1, 0).wait_recv()
    for one in started:
        one.wait_send()


def cube_scatter(me, parts, got1, sums, got2, got3, total, send1, recv1, send2, recv2, send3, recv3):
    half_rows = parts.shape[1] // 2
    firsts = ((2, 4), (4, 2))

    def rows_of(half):
        return pl.ds(half * half_rows, half_rows)

    def one_copy(src, dst, send, recv, flip):
        return pltpu.make_async_remote_copy(
            src_ref=src,
            dst_ref=dst,
            send_sem=send,
            recv_sem=recv,
            device_id={"dp": me ^ flip},
            device_id_type=MESH,
        )

    first_copies = {}
    for slot in (3, 1, 2, 0):
        first_copies[slot] = one_copy(
            parts.at[me ^ 1 ^ (2 * slot)], got1.at[slot], send1.at[slot], recv1.at[slot], 1
        )
        first_copies[slot].start()
    yield
    second_copies = {}
    for slot in (3, 1, 2, 0):
        first_copies[slot].wait_recv()
        sums[slot] = (
            parts[me ^ (2 * slot)].astype(jnp.float32) + got1[slot].astype(jnp.float32)
        ).astype(sums.dtype)
        for half in range(2):
            first, second = firsts[half]
            if slot == 3 or slot == first // 2:
                goes = 1 if slot == 3 else 0
                second_copies[half, goes] = one_copy(
                    sums.at[slot, rows_of(half)],
                    got2.at[half, goes],
                    send2.at[half, goes],
                    recv2.at[half, goes],
                    first,
                )
                second_copies[half, goes].start()
    yield
    third_copies = {}
    for half in range(2):
        first, second = firsts[half]
        second_copies[half, 1].wait_recv()
        slot = second // 2
        sums[slot, rows_of(half)] = (
            sums[slot, rows_of(half)].astype(jnp.float32) + got2[half, 1].astype(jnp.float32)
        ).astype(sums.dtype)
        third_copies[half] = one_copy(
            sums.at[slot, rows_of(half)], got3.at[half], send3.at[half], recv3.at[half], second
        )
        third_copies[half].start()
    yield
    for half in range(2):
        second_copies[half, 0].wait_recv()
        total[rows_of(half)] = sums[0, rows_of(half)].astype(jnp.float32) + got2[half, 0].astype(
            jnp.float32
        )
    yield
    for half in range(2):
        third_copies[half].wait_recv()
        total[rows_of(half)] = total[rows_of(half)] + got3[half].astype(jnp.float32)
    for group in (first_copies, second_copies, third_copies):
        for one in group.values():
            one.wait_send()


def norm_forward(values, gain_row):
    inv_root = lax.rsqrt(jnp.mean(values * values, axis=-1, keepdims=True) + EPS)
    return values * inv_root * gain_row


def norm_backward(grad_out, values, gain_row):
    inv_root = lax.rsqrt(jnp.mean(values * values, axis=-1, keepdims=True) + EPS)
    normal = values * inv_root
    scaled = grad_out * gain_row
    values_grad = inv_root * (scaled - normal * jnp.mean(scaled * normal, axis=-1, keepdims=True))
    return (values_grad, jnp.sum(grad_out * normal, axis=0, keepdims=True))


def own_rows(pos, buf, count):
    rows = buf.shape[1] // count
    return pl.ds(pl.multiple_of(pos * rows, rows), rows)


def scatter_scratch(shape):
    return [
        pltpu.VMEM((2,) + shape, jnp.bfloat16),
        pltpu.VMEM((2,) + shape, jnp.bfloat16),
    ]


def scatter_sems(count, micro):
    return [
        pltpu.SemaphoreType.DMA((2, count, micro)),
        pltpu.SemaphoreType.DMA((2, count, micro)),
    ]


def gather_sems(count, micro):
    return [
        pltpu.SemaphoreType.DMA((2, count, micro)),
        pltpu.SemaphoreType.DMA((count, micro)),
    ]


def call(kernel, outs, scratch, ident, name, *args):
    return pl.pallas_call(
        kernel,
        out_shape=[jax.ShapeDtypeStruct(shape, kind) for shape, kind in outs],
        in_specs=[pl.BlockSpec(memory_space=pltpu.VMEM)] * len(args),
        out_specs=[pl.BlockSpec(memory_space=pltpu.VMEM)] * len(outs),
        scratch_shapes=scratch,
        compiler_params=pltpu.CompilerParams(
            collective_id=ident, has_side_effects=True, vmem_limit_bytes=VMEM_LIMIT
        ),
        name=name,
    )(*args)


def entry_kernel(count, with_cube, *refs):
    if with_cube:
        weights, refs = refs[0], refs[1:]
    rows_in, refs = refs[:2], refs[2:]
    if with_cube:
        weights_all, refs = refs[0], refs[1:]
    rows_out, refs = refs[:2], refs[2:]
    pos = lax.axis_index("tensor")
    me = lax.axis_index("dp") if with_cube else None
    for source, target in zip(rows_in, rows_out):
        for step in range(source.shape[0]):
            target[step, own_rows(pos, target, count)] = source[step]
    if with_cube:
        weights_all[me] = weights[...]
    greet(pos, count, me)
    streams = []
    if with_cube:
        streams.append(cube_gather(me, weights_all, refs[4], refs[5]))
    for which in range(2):
        streams.append(
            line_gather(pos, count, rows_out[which], refs[2 * which], refs[2 * which + 1])
        )
    run_together(*streams)


def forward_kernel(count, beside, *refs):
    parts, resid, gain = refs[:3]
    refs = refs[3:]
    if beside:
        extra, refs = refs[0], refs[1:]
    total_out, normed_all = refs[:2]
    refs = refs[2:]
    if beside:
        extra_all, refs = refs[0], refs[1:]
    got, staged, s_send, s_recv, g_send, g_recv = refs[:6]
    pos = lax.axis_index("tensor")
    me = lax.axis_index("dp") if beside == "cube" else None
    streams = []
    if beside == "cube":
        extra_all[me] = extra[...]
    if beside == "line":
        for step in range(extra.shape[0]):
            extra_all[step, own_rows(pos, extra_all, count)] = extra[step]
    greet(pos, count, me)

    def main(step):
        yield from line_scatter(
            pos, count, parts, got, staged, total_out, s_send, s_recv, (step,)
        )
        total = total_out[step] + resid[step].astype(jnp.float32)
        total_out[step] = total
        normed_all[step, own_rows(pos, normed_all, count)] = norm_forward(
            total, gain[...]
        ).astype(jnp.bfloat16)
        yield from line_gather(pos, count, normed_all, g_send, g_recv, (step,))

    for step in range(parts.shape[0]):
        streams.append(main(step))
    if beside == "cube":
        streams.append(cube_gather(me, extra_all, refs[6], refs[7]))
    if beside == "line":
        streams.append(line_gather(pos, count, extra_all, refs[6], refs[7]))
    run_together(*streams)


def back_kernel(count, side_kind, cubes, *refs):
    parts, side_parts, values, gain, grad_in, side_resid = refs[:6]
    refs = refs[6:]
    weight_parts, refs = refs[:cubes], refs[cubes:]
    grad_out, gathered, side_out, gain_out = refs[:4]
    refs = refs[4:]
    weight_out, refs = refs[:cubes], refs[cubes:]
    got, staged, side_got, side_staged, side_total = refs[:5]
    s_send, s_recv, t_send, t_recv, g_send, g_recv = refs[5:11]
    refs = refs[11:]
    pos = lax.axis_index("tensor")
    me = lax.axis_index("dp") if cubes else None
    greet(pos, count, me)

    gain_out[...] = jnp.zeros_like(gain_out)

    def main(step):
        yield from line_scatter(
            pos, count, parts, got, staged, grad_out, s_send, s_recv, (step,)
        )
        moved, gain_part = norm_backward(grad_out[step], values[step], gain[...])
        total = grad_in[step].astype(jnp.float32) + moved
        grad_out[step] = total
        gain_out[...] = gain_out[...] + gain_part
        gathered[step, own_rows(pos, gathered, count)] = total.astype(jnp.bfloat16)
        yield from line_gather(pos, count, gathered, g_send, g_recv, (step,))

    def side():
        yield from line_scatter(
            pos, count, side_parts, side_got, side_staged, side_total, t_send, t_recv
        )
        for step in range(parts.shape[0]):
            if side_kind == "out":
                side_out[step] = (side_total[step] + side_resid[step]).astype(jnp.bfloat16)
            else:
                side_out[step] = side_total[step]

    run_together(*[main(step) for step in range(parts.shape[0])], side(), *cube_streams(me, weight_parts, weight_out, refs))


def cube_streams(me, weight_parts, weight_out, refs):
    return [
        cube_scatter(
            me,
            weight_parts[which],
            *refs[10 * which : 10 * which + 4],
            weight_out[which],
            *refs[10 * which + 4 : 10 * which + 10],
        )
        for which in range(len(weight_parts))
    ]


def cube_scratch(shard_rows, columns):
    return [
        pltpu.VMEM((4, shard_rows, columns), jnp.bfloat16),
        pltpu.VMEM((4, shard_rows, columns), jnp.bfloat16),
        pltpu.VMEM((2, 2, shard_rows // 2, columns), jnp.bfloat16),
        pltpu.VMEM((2, shard_rows // 2, columns), jnp.bfloat16),
        pltpu.SemaphoreType.DMA((4,)),
        pltpu.SemaphoreType.DMA((4,)),
        pltpu.SemaphoreType.DMA((2, 2)),
        pltpu.SemaphoreType.DMA((2, 2)),
        pltpu.SemaphoreType.DMA((2,)),
        pltpu.SemaphoreType.DMA((2,)),
    ]


def exit_kernel(count, cubes, *refs):
    parts, values, gain, grad_in, small = refs[:5]
    refs = refs[5:]
    weight_parts, refs = refs[:cubes], refs[cubes:]
    grad_out, small_out = refs[:2]
    refs = refs[2:]
    weight_out, refs = refs[:cubes], refs[cubes:]
    got, staged, s_send, s_recv = refs[:4]
    refs = refs[4:]
    pos = lax.axis_index("tensor")
    me = lax.axis_index("dp") if cubes else None
    greet(pos, count, me)

    small_out[...] = small[...]

    def main(step):
        yield from line_scatter(
            pos, count, parts, got, staged, grad_out, s_send, s_recv, (step,)
        )
        moved, gain_part = norm_backward(
            grad_out[step], values[step].astype(jnp.float32), gain[...]
        )
        grad_out[step] = grad_in[step] + moved
        small_out[0:1] = small_out[0:1] + gain_part

    run_together(*[main(step) for step in range(parts.shape[0])], *cube_streams(me, weight_parts, weight_out, refs))
    if cubes:
        small_sum(pos, count, me, small_out, *refs[10 * cubes :])


def dot_plain(left, right):
    return jnp.dot(left, right, preferred_element_type=jnp.float32)


def dot_left_t(left, right):
    return lax.dot_general(
        left, right, (((0,), (0,)), ((), ())), preferred_element_type=jnp.float32
    )


def dot_right_t(left, right):
    return lax.dot_general(
        left, right, (((1,), (1,)), ((), ())), preferred_element_type=jnp.float32
    )


def gelu_tanh(values):
    return jax.nn.gelu(values, approximate=True)


def head_split(values, heads_local):
    return values.reshape(values.shape[:2] + (heads_local, values.shape[2] // heads_local))


def attend_forward(query_rows, key_rows, value_rows, heads_local, extra, allowed):
    scores = (
        jnp.einsum(
            "bqhd,bkhd->bhqk",
            head_split(query_rows, heads_local),
            head_split(key_rows, heads_local),
            preferred_element_type=jnp.float32,
        )
        + extra
    )
    scores = jnp.where(allowed[:, None], scores, NEG)
    biggest = jnp.max(scores, axis=-1, keepdims=True)
    exponent = jnp.exp(scores - biggest)
    probs = exponent / jnp.sum(exponent, axis=-1, keepdims=True)
    mixed = jnp.einsum(
        "bhqk,bkhd->bqhd",
        probs.astype(jnp.bfloat16),
        head_split(value_rows, heads_local),
        preferred_element_type=jnp.float32,
    )
    return (mixed.reshape(query_rows.shape).astype(jnp.bfloat16), probs)


def attend_backward(query_rows, key_rows, value_rows, heads_local, probs, mixed_grad):
    grad_heads = head_split(mixed_grad, heads_local)
    query_heads = head_split(query_rows, heads_local)
    key_heads = head_split(key_rows, heads_local)
    prob_grad = jnp.einsum(
        "bqhd,bkhd->bhqk",
        grad_heads,
        head_split(value_rows, heads_local),
        preferred_element_type=jnp.float32,
    )
    score_low = (probs * (prob_grad - jnp.sum(probs * prob_grad, axis=-1, keepdims=True))).astype(
        jnp.bfloat16
    )
    query_grad = jnp.einsum(
        "bhqk,bkhd->bqhd", score_low, key_heads, preferred_element_type=jnp.float32
    )
    key_grad = jnp.einsum(
        "bhqk,bqhd->bkhd", score_low, query_heads, preferred_element_type=jnp.float32
    )
    value_grad = jnp.einsum(
        "bhqk,bqhd->bkhd", probs.astype(jnp.bfloat16), grad_heads, preferred_element_type=jnp.float32
    )
    return (
        query_grad.reshape(query_rows.shape).astype(jnp.bfloat16),
        key_grad.reshape(key_rows.shape).astype(jnp.bfloat16),
        value_grad.reshape(key_rows.shape).astype(jnp.bfloat16),
        score_low,
    )


def rows_dot(rows, matrix):
    return lax.dot_general(
        rows, matrix, (((2,), (0,)), ((), ())), preferred_element_type=jnp.float32
    )


def rows_dot_t(rows, matrix):
    return lax.dot_general(
        rows, matrix, (((2,), (1,)), ((), ())), preferred_element_type=jnp.float32
    )


def weight_dot(left, right):
    return dot_left_t(
        left.reshape(-1, left.shape[-1]), right.reshape(-1, right.shape[-1])
    ).astype(jnp.bfloat16)

def bias_kernel(rows, out):
    length = out.shape[1]
    for head in range(out.shape[0]):
        out[head] = pltpu.roll(
            jnp.broadcast_to(rows[head : head + 1], (length, length)), 0, 1, stride=1, stride_axis=0
        )


def diagonal_kernel(scores, out):
    length = scores.shape[2]
    turned = (
        lax.broadcasted_iota(jnp.int32, (length, length), 0)
        + lax.broadcasted_iota(jnp.int32, (length, length), 1)
        == length - 1
    ).astype(jnp.bfloat16)
    for head in range(scores.shape[1]):
        flipped = jnp.dot(turned, scores[0, head], preferred_element_type=jnp.float32)
        for step in range(1, scores.shape[0]):
            flipped = flipped + jnp.dot(
                turned, scores[step, head], preferred_element_type=jnp.float32
            )
        moved = pltpu.roll(flipped, 1, 1, stride=1, stride_axis=0)
        out[head : head + 1] = jnp.sum(moved, axis=0, keepdims=True)


def local_call(kernel, shape, name, arg):
    return pl.pallas_call(
        kernel,
        out_shape=jax.ShapeDtypeStruct(shape, jnp.float32),
        in_specs=[pl.BlockSpec(memory_space=pltpu.VMEM)],
        out_specs=pl.BlockSpec(memory_space=pltpu.VMEM),
        compiler_params=pltpu.CompilerParams(vmem_limit_bytes=VMEM_LIMIT),
        name=name,
    )(arg)


def body(
    tokens,
    encoder,
    cotangent,
    dec_segments,
    enc_segments,
    buckets,
    self_query,
    self_key,
    self_value,
    self_output,
    cross_query,
    cross_key,
    cross_value,
    cross_output,
    gate_weight,
    up_weight,
    down_weight,
    gain_self,
    gain_cross,
    gain_feed,
    bias_table,
):
    low = jnp.bfloat16
    dp_count = lax.axis_size("dp")
    count = lax.axis_size("tensor")
    heads_local = bias_table.shape[1]
    inner = self_query.shape[1]
    hidden_local = gate_weight.shape[1]
    shard_rows = self_query.shape[0]
    width = shard_rows * dp_count
    micro, row_count = tokens.shape[:2]
    seq_len = row_count * count
    enc_len = encoder.shape[1] * count
    with_cube = dp_count == CUBE and shard_rows % 32 == 0

    gain_columns = jnp.pad(
        jnp.stack([gain_self, gain_cross, gain_feed], axis=1), ((0, 0), (0, 125))
    )
    packed = jnp.concatenate(
        [
            self_query,
            self_key,
            self_value,
            cross_query,
            cross_key,
            cross_value,
            self_output.T,
            cross_output.T,
            gain_columns,
        ],
        axis=1,
    )
    packed_feed = jnp.concatenate([gate_weight, up_weight, down_weight.T], axis=1)
    cube_sems = [pltpu.SemaphoreType.DMA((8, 2)), pltpu.SemaphoreType.DMA((CUBE, 2))]
    rows_shape = (micro, seq_len, width)
    enc_shape = (micro, enc_len, width)
    own_shape = (micro, row_count, width)
    line_sems = gather_sems(count, micro)
    entry_args = [tokens, encoder]
    entry_outs = [(rows_shape, low), (enc_shape, low)]
    entry_scratch = line_sems * 2
    if with_cube:
        entry_args.insert(0, packed)
        entry_outs.insert(0, ((CUBE,) + packed.shape, low))
        entry_scratch = entry_scratch + cube_sems
    entry = call(
        functools.partial(entry_kernel, count, with_cube),
        entry_outs,
        entry_scratch,
        0,
        "entry_gather",
        *entry_args,
    )
    if with_cube:
        whole, tokens_all, encoder_all = entry
        whole = whole.reshape(width, packed.shape[1])
    else:
        tokens_all, encoder_all = entry
        whole = lax.all_gather(packed, "dp", axis=0, tiled=True)
    base = 0
    w_qkv = whole[:, base : base + 3 * inner]
    w_cq = whole[:, base + 3 * inner : base + 4 * inner]
    w_ckv = whole[:, base + 4 * inner : base + 6 * inner]
    w_so_t = whole[:, base + 6 * inner : base + 7 * inner]
    w_co_t = whole[:, base + 7 * inner : base + 8 * inner]
    gains = whole[:, base + 8 * inner : base + 8 * inner + 3].T.astype(jnp.float32)
    gain1, gain2, gain3 = gains[0:1], gains[1:2], gains[2:3]

    position = jnp.arange(seq_len, dtype=jnp.int32)
    causal = position[:, None] >= position[None, :]
    buckets_back = jnp.concatenate([buckets[:1], buckets[1:][::-1]])
    hits_back = buckets_back[:, None] == jnp.arange(BUCKETS, dtype=jnp.int32)[None, :]
    bias_rows = lax.dot_general(
        bias_table, hits_back.astype(low), (((0,), (1,)), ((), ())), preferred_element_type=jnp.float32
    )
    bias_full = local_call(
        bias_kernel, (heads_local, seq_len, seq_len), "bias_spread", bias_rows
    )
    dec_seg = dec_segments[:, 0]
    enc_seg = enc_segments[:, 0]
    self_allowed = causal[None] & (dec_seg[:, :, None] == dec_seg[:, None, :])
    cross_allowed = dec_seg[:, :, None] == enc_seg[:, None, :]

    forward_scratch = (
        scatter_scratch(rows_shape) + scatter_sems(count, micro) + gather_sems(count, micro)
    )
    normed1_all = norm_forward(tokens_all.astype(jnp.float32), gain1).astype(low)
    qkv = rows_dot(normed1_all, w_qkv).astype(low)
    query1, key1, value1 = (
        qkv[..., :inner],
        qkv[..., inner : 2 * inner],
        qkv[..., 2 * inner :],
    )
    mixed1, probs1 = attend_forward(query1, key1, value1, heads_local, bias_full, self_allowed)
    self_args = [rows_dot_t(mixed1, w_so_t).astype(low), tokens, gain2]
    self_outs = [(own_shape, jnp.float32), (rows_shape, low)]
    if with_cube:
        self_args.append(packed_feed)
        self_outs.append(((CUBE,) + packed_feed.shape, low))
    self_ended = call(
        functools.partial(forward_kernel, count, "cube" if with_cube else ""),
        self_outs,
        forward_scratch + (cube_sems if with_cube else []),
        1,
        "self_sum_norm",
        *self_args,
    )
    if with_cube:
        first, normed2_all, feed_whole = self_ended
        feed_whole = feed_whole.reshape(width, packed_feed.shape[1])
    else:
        first, normed2_all = self_ended
        feed_whole = lax.all_gather(packed_feed, "dp", axis=0, tiled=True)
    w_gate_up = feed_whole[:, : 2 * hidden_local]
    w_down_t = feed_whole[:, 2 * hidden_local :]
    key_value2 = rows_dot(encoder_all, w_ckv).astype(low)
    key2, value2 = key_value2[..., :inner], key_value2[..., inner:]
    query2 = rows_dot(normed2_all, w_cq).astype(low)
    mixed2, probs2 = attend_forward(query2, key2, value2, heads_local, 0.0, cross_allowed)
    second, normed3_all, cot_all = call(
        functools.partial(forward_kernel, count, "line"),
        [(own_shape, jnp.float32), (rows_shape, low), (rows_shape, low)],
        forward_scratch + gather_sems(count, micro),
        2,
        "cross_sum_norm",
        rows_dot_t(mixed2, w_co_t).astype(low),
        first,
        gain3,
        cotangent,
    )
    gate_up = rows_dot(normed3_all, w_gate_up)
    gate_pre, up_pre = gate_up[..., :hidden_local], gate_up[..., hidden_local:]
    gate_act, gate_pull = jax.vjp(gelu_tanh, gate_pre)
    hidden = (gate_act * up_pre).astype(low)
    hidden_grad = rows_dot(cot_all, w_down_t)
    gate_grad = gate_pull(hidden_grad * up_pre)[0].astype(low)
    up_grad = (hidden_grad * gate_act).astype(low)
    gate_up_grad = jnp.concatenate([gate_grad, up_grad], axis=-1)

    def back_scratch(side_shape, side_own):
        return (
            scatter_scratch(rows_shape)
            + scatter_scratch(side_shape)
            + [pltpu.VMEM(side_own, jnp.float32)]
            + scatter_sems(count, micro) * 2
            + gather_sems(count, micro)
        )

    second_grad, cross_out_all, layer_out, gain3_part = call(
        functools.partial(back_kernel, count, "out", 0),
        [
            (own_shape, jnp.float32),
            (rows_shape, low),
            (own_shape, low),
            ((1, width), jnp.float32),
        ],
        back_scratch(rows_shape, own_shape),
        3,
        "feed_back",
        rows_dot_t(gate_up_grad, w_gate_up).astype(low),
        rows_dot_t(hidden, w_down_t).astype(low),
        second,
        gain3,
        cotangent,
        second,
    )
    mixed2_grad = rows_dot(cross_out_all, w_co_t).astype(low)
    query2_grad, key2_grad, value2_grad, score2_low = attend_backward(
        query2, key2, value2, heads_local, probs2, mixed2_grad
    )
    key_value2_grad = jnp.concatenate([key2_grad, value2_grad], axis=-1)
    enc_own = (micro, encoder.shape[1], width)
    feed_parts = [
        weight_dot(normed3_all, gate_up_grad),
        weight_dot(cot_all, hidden),
    ]

    def cube_args(parts):
        return [one.reshape(CUBE, shard_rows, one.shape[1]) for one in parts] if with_cube else []

    def cube_outs(parts):
        return [((shard_rows, one.shape[1]), jnp.float32) for one in parts] if with_cube else []

    def cube_space(parts):
        scratch = []
        if with_cube:
            for one in parts:
                scratch = scratch + cube_scratch(shard_rows, one.shape[1])
        return scratch

    def owned_parts(ended, parts):
        if with_cube:
            return ended
        return [
            lax.psum_scatter(one.astype(jnp.float32), "dp", scatter_dimension=0, tiled=True)
            for one in parts
        ]

    first_grad, self_out_all, encoder_grad, gain2_part, *feed_ended = call(
        functools.partial(back_kernel, count, "plain", len(cube_args(feed_parts))),
        [
            (own_shape, jnp.float32),
            (rows_shape, low),
            (enc_own, jnp.float32),
            ((1, width), jnp.float32),
        ]
        + cube_outs(feed_parts),
        back_scratch(enc_shape, enc_own) + cube_space(feed_parts),
        4,
        "cross_back",
        rows_dot_t(query2_grad, w_cq).astype(low),
        rows_dot_t(key_value2_grad, w_ckv).astype(low),
        first,
        gain2,
        second_grad,
        second,
        *cube_args(feed_parts),
    )
    mixed1_grad = rows_dot(self_out_all, w_so_t).astype(low)
    query1_grad, key1_grad, value1_grad, score1_low = attend_backward(
        query1, key1, value1, heads_local, probs1, mixed1_grad
    )
    qkv_grad = jnp.concatenate([query1_grad, key1_grad, value1_grad], axis=-1)
    head_parts = [
        weight_dot(normed1_all, qkv_grad),
        jnp.concatenate(
            [
                weight_dot(normed2_all, query2_grad),
                weight_dot(encoder_all, key_value2_grad),
                weight_dot(self_out_all, mixed1),
                weight_dot(cross_out_all, mixed2),
            ],
            axis=1,
        ),
    ]
    per_distance = local_call(
        diagonal_kernel, (heads_local, seq_len), "diagonal_sums", score1_low
    )
    tables = lax.dot_general(
        hits_back.astype(jnp.float32),
        per_distance,
        (((0,), (1,)), ((), ())),
        precision=lax.Precision.HIGHEST,
        preferred_element_type=jnp.float32,
    )
    pos = lax.axis_index("tensor")
    table_size = tables.shape[0] * tables.shape[1]
    placed_table = jnp.where(
        (jnp.arange(count, dtype=jnp.int32) == pos)[:, None], tables.reshape(1, -1), 0.0
    ).reshape(1, -1)
    small = jnp.concatenate(
        [
            jnp.zeros((1, width), jnp.float32),
            gain2_part,
            gain3_part,
            jnp.pad(placed_table, ((0, 0), (0, width - count * table_size))),
            jnp.zeros((4, width), jnp.float32),
        ],
        axis=0,
    )
    exit_scratch = (
        scatter_scratch(rows_shape) + scatter_sems(count, micro) + cube_space(head_parts)
    )
    if with_cube:
        exit_scratch = exit_scratch + [
            pltpu.VMEM((3,) + small.shape, jnp.float32),
            pltpu.VMEM((count - 1,) + small.shape, jnp.float32),
            pltpu.SemaphoreType.DMA((3,)),
            pltpu.SemaphoreType.DMA((3,)),
            pltpu.SemaphoreType.DMA((count - 1,)),
            pltpu.SemaphoreType.DMA((count - 1,)),
        ]
    token_grad, small_out, *head_ended = call(
        functools.partial(exit_kernel, count, len(cube_args(head_parts))),
        [(own_shape, jnp.float32), (small.shape, jnp.float32)] + cube_outs(head_parts),
        exit_scratch,
        5,
        "exit_sums",
        rows_dot_t(qkv_grad, w_qkv).astype(low),
        tokens,
        gain1,
        first_grad,
        small,
        *cube_args(head_parts),
    )
    if not with_cube:
        small_out = lax.psum(small_out, ("dp", "tensor"))
    gate_up_owned, down_owned = owned_parts(feed_ended, feed_parts)
    qkv_owned, others = owned_parts(head_ended, head_parts)
    index = lax.axis_index("dp") * count + pos
    piece = width // (dp_count * count)
    gain_grads = tuple(
        lax.dynamic_slice(small_out, (which, index * piece), (1, piece)).reshape(-1)
        for which in range(3)
    )
    table_grad = lax.dynamic_slice(small_out, (3, pos * table_size), (1, table_size)).reshape(
        tables.shape
    )

    return (
        layer_out,
        token_grad,
        encoder_grad,
        qkv_owned[:, :inner],
        qkv_owned[:, inner : 2 * inner],
        qkv_owned[:, 2 * inner :],
        others[:, 3 * inner : 4 * inner].T,
        others[:, :inner],
        others[:, inner : 2 * inner],
        others[:, 2 * inner : 3 * inner],
        others[:, 4 * inner :].T,
        gate_up_owned[:, :hidden_local],
        gate_up_owned[:, hidden_local:],
        down_owned.T,
    ) + gain_grads + (table_grad,)


def solution(mesh):
    placed = (
        P(None, ("dp", "tensor"), None),
        P(None, ("dp", "tensor"), None),
        P(None, ("dp", "tensor"), None),
        P(None, "dp", None),
        P(None, "dp", None),
        P(),
        P("dp", "tensor"),
        P("dp", "tensor"),
        P("dp", "tensor"),
        P("tensor", "dp"),
        P("dp", "tensor"),
        P("dp", "tensor"),
        P("dp", "tensor"),
        P("tensor", "dp"),
        P("dp", "tensor"),
        P("dp", "tensor"),
        P("tensor", "dp"),
        P("dp"),
        P("dp"),
        P("dp"),
        P(None, "tensor"),
    )
    return jax.shard_map(
        body,
        mesh=mesh,
        in_specs=placed,
        out_specs=(
            P(None, ("dp", "tensor"), None),
            P(None, ("dp", "tensor"), None),
            P(None, ("dp", "tensor"), None),
            P("dp", "tensor"),
            P("dp", "tensor"),
            P("dp", "tensor"),
            P("tensor", "dp"),
            P("dp", "tensor"),
            P("dp", "tensor"),
            P("dp", "tensor"),
            P("tensor", "dp"),
            P("dp", "tensor"),
            P("dp", "tensor"),
            P("tensor", "dp"),
            P(("dp", "tensor")),
            P(("dp", "tensor")),
            P(("dp", "tensor")),
            P(None, "tensor"),
        ),
        check_vma=False,
    )
```
